512 devices in a mesh: cells: 64 (over x, z, core), grp: 8 (over y).
Axes of the slice: x: 4, y: 8, z: 8, core: 2. Of those that a mesh axis runs over, the one named last changes fastest.
Arguments:
- ensemble: float32 [128, 262144], P('grp', 'cells'), may hold values from -6 to 6
- gauge_owner: int32 [2, 512, 1], replicated, may hold values from 0 to 63; in each aligned block of 512 rows (0 to 511, 512 to 1023, ..., all dimensions but the last counted through in order) at most 24 rows name the same one
- gauge_block: int32 [2, 512], replicated, may hold values from 0 to 31
- gauge_weight: float32 [2, 512, 128], replicated, may hold values from -0.5 to 0.5
- gauge_value: float32 [2, 512], replicated, may hold values from -6 to 6
- gauge_error: float32 [2, 512], replicated, may hold values from 0.5 to 4
- loc_level: int32 [2, 2048], P(None, 'cells'), may hold values from 0 to 4
Outputs:
- analysis: float32 [128, 262144], P('grp', 'cells')
The draws below stay inside these ranges and needn't reach their ends.
Inputs may be any that keep to these rules, and one draw needn't show every extreme that they name: `gauge_owner`: in each batch no index of cells owns more than 24 gauges, and some index owns exactly 24.
All inputs are finite; a program needn't handle non-finite values.
Results may differ from the reference program's by a relative error of at most 0.0001.
Values sent between devices are 32-bit elements; how exact they have to be, the bound alone decides.
A program may use at most 64 MiB of HBM per device.

```python
import math
import jax
import jax.numpy as jnp
import numpy as np
from jax import lax

M = 128
BLK = 128
NBLK_DEV = 32
NBATCH = 2
NSIT = 12
CAP = 24
P_SIZE = 512
NBLK = 2048
NC = 262144
N_CELLS = 64


def with_ends(entries, key, low, top_value):
    longest = entries.shape.index(max(entries.shape))
    spots = []
    for shift in (0, 1):
        where = [jax.random.randint(jax.random.fold_in(key, axis), (), 0, length) for axis, length in enumerate(entries.shape)]
        where[longest] = (where[longest] + shift) % entries.shape[longest]
        spots.append(tuple(where))
    return entries.at[spots[0]].set(low).at[spots[1]].set(top_value)


def levels(key, shape, split, least, high):
    def one(position, blocks):
        heights = jax.random.uniform(jax.random.fold_in(jax.random.fold_in(key, 6), position), (blocks,), jnp.float32, least / len(split), high / len(split))
        return jnp.repeat(jnp.exp(heights), shape[position] // blocks).reshape((-1,) + (1,) * (len(shape) - position - 1))

    factor_of = one(*split[0])
    for cut in split[1:]:
        factor_of = factor_of * one(*cut)
    return factor_of


def routed_block(own_key, own, number, rows, number_of, top, limit, slope):
    ranking = jax.random.permutation(own_key, number_of)
    packed, common = load_shares(number_of, rows * top, limit, slope, True), load_shares(number_of, rows * top, limit, slope, False)
    places = jnp.arange(number_of)

    def named(sizes, turn):
        used = int((sizes > 0).sum())
        fixed = max(1, used // 4)
        moved = fixed + (places - fixed + turn * (used - fixed)) % max(1, number_of - fixed)
        return jnp.zeros((number_of,), jnp.int32).at[ranking[jnp.where(places < fixed, places, moved)]].set(jnp.asarray(sizes, jnp.int32))

    sizes = jnp.where(number % 4 == 0, named(packed, number // 4), named(common, number - number // 4 - 1))
    mixed = jax.random.permutation(jax.random.fold_in(own, 3), number_of)
    source_of, taker = mixed[0:number_of // 2 * 2:2], mixed[1:number_of // 2 * 2:2]
    margin = jnp.minimum(sizes[source_of] - 1, limit - sizes[taker]) // 2
    margin = jnp.where((source_of == ranking[0]) | (taker == ranking[0]) | (sizes[taker] == 0), 0, jnp.maximum(margin, 0))
    moved = jax.random.randint(jax.random.fold_in(own, 4), (number_of // 2,), 0, 1 << 20) % (margin + 1)
    sizes = sizes.at[source_of].add(-moved).at[taker].add(moved)
    members = jnp.searchsorted(jnp.cumsum(sizes), jnp.arange(rows * top), side="right").astype(jnp.int32)
    listing = members.reshape(top, rows).T
    listing = listing[jax.random.permutation(jax.random.fold_in(own, 1), rows)]
    turn = jax.random.randint(jax.random.fold_in(own, 2), (rows, 1), 0, top)
    return jnp.take_along_axis(listing, (jnp.arange(top)[None, :] + turn) % top, axis=1)


def load_shares(amount, total, reach, lean, full):
    portions = [(1 << 20) // math.isqrt(rank ** lean) + 1 for rank in range(1, amount + 1)]
    largest = reach if full else min(reach, max(-(-total // amount), total * portions[0] // sum(portions)))
    least = 1 if total - largest >= amount - 1 else 0
    holding, surplus = [largest] + [least] * (amount - 1), total - largest - least * (amount - 1)
    while surplus > 0:
        candidates = [i for i in range(1, amount) if holding[i] < largest] or [i for i in range(1, amount) if holding[i] < reach]
        mass, remaining = sum([portions[i] for i in candidates]), surplus
        for i in candidates:
            more = min(reach - holding[i], max(1, remaining * portions[i] // mass), surplus)
            holding[i] = holding[i] + more
            surplus = surplus - more
    return np.array(holding)


def centred(stream_key, dims, deviation, reach, split=(), held_as=jnp.bfloat16):
    values = jax.random.normal(stream_key, dims, jnp.float32) * deviation
    if len(split) > 0:
        values = levels(stream_key, dims, split, -0.22, 0.18) * values
    return jnp.clip(values, min=-reach, max=reach).astype(held_as)


def setup_inputs(seed: int = 0) -> dict:
    streams_of = jax.random.split(jax.random.key(seed), 8)
    ensemble = centred(streams_of[0], (M, NC), 1.0, 6.0, ((0, 8), (1, 64)), jnp.float32)
    gauge_owner_keys = jax.random.split(jax.random.fold_in(streams_of[1], 1), NBATCH * P_SIZE // P_SIZE)
    gauge_owner_turns = jax.random.permutation(jax.random.fold_in(streams_of[1], 3), NBATCH * P_SIZE // P_SIZE)
    gauge_owner = jax.vmap(lambda own, number: routed_block(jax.random.fold_in(streams_of[1], 2), own, number, P_SIZE, N_CELLS, 1, CAP, 2))(gauge_owner_keys, gauge_owner_turns).reshape((NBATCH, P_SIZE, 1))
    gauge_block = with_ends(jax.random.randint(streams_of[2], (NBATCH, P_SIZE), 0, NBLK_DEV), jax.random.fold_in(streams_of[2], 1), 0, NBLK_DEV - 1).astype(jnp.int32)
    gauge_weight = centred(streams_of[3], (NBATCH, P_SIZE, BLK), BLK ** -0.5, 0.5, (), jnp.float32)
    gauge_value = centred(streams_of[4], (NBATCH, P_SIZE), 1.0, 6.0, (), jnp.float32)
    gauge_error = jnp.clip(jnp.exp(jax.random.uniform(streams_of[5], (NBATCH, P_SIZE), jnp.float32, math.log(0.5), math.log(4.0))), 0.5, 4.0)
    loc_level = with_ends(jax.random.randint(streams_of[6], (NBATCH, NBLK), 0, 5), jax.random.fold_in(streams_of[6], 1), 0, 4).astype(jnp.int32)
    return {"ensemble": ensemble, "gauge_owner": gauge_owner, "gauge_block": gauge_block, "gauge_weight": gauge_weight, "gauge_value": gauge_value, "gauge_error": gauge_error, "loc_level": loc_level}


def make_transform(gram, bvec):
    order = gram.shape[0]
    identity = jnp.eye(order, dtype=jnp.float32)
    amat = identity + gram
    lower = jnp.linalg.cholesky(amat)
    middle = lax.linalg.triangular_solve(lower, bvec[:, None], left_side=True, lower=True)
    wbar = lax.linalg.triangular_solve(lower, middle, left_side=True, lower=True, transpose_a=True)[:, 0]
    scal = jnp.trace(amat)

    def newton(index, carry):
        ymat, zmat = carry
        qmat = 1.5 * identity - 0.5 * jnp.dot(zmat, ymat, precision=lax.Precision.HIGHEST)
        return (jnp.dot(ymat, qmat, precision=lax.Precision.HIGHEST), jnp.dot(qmat, zmat, precision=lax.Precision.HIGHEST))
    ymat, zmat = lax.fori_loop(0, NSIT, newton, (amat / scal, identity))
    sqinv = zmat / jnp.sqrt(scal)
    return sqinv + wbar[:, None] / jnp.sqrt(jnp.float32(order - 1)) - identity

def reference(ensemble, gauge_owner, gauge_block, gauge_weight, gauge_value, gauge_error, loc_level):
    state = ensemble
    scale = jnp.sqrt(jnp.float32(M - 1))
    for batch in range(NBATCH):
        blocked = state.reshape(M, NBLK, BLK)
        where_idx = (gauge_owner[batch, :, 0] * NBLK_DEV + gauge_block[batch]).astype(jnp.int32)
        picked = blocked[:, where_idx, :]
        prior = jnp.einsum('mpc,pc->mp', picked, gauge_weight[batch], precision=lax.Precision.HIGHEST)
        ymean = lax.optimization_barrier(jnp.mean(prior, axis=0))
        smat = ((prior - ymean[None, :]) / (gauge_error[batch][None, :] * scale)).T
        dvec = (gauge_value[batch] - ymean) / gauge_error[batch]
        gram = jnp.dot(smat.T, smat, precision=lax.Precision.HIGHEST)
        bvec = jnp.dot(smat.T, dvec, precision=lax.Precision.HIGHEST)
        mixer = make_transform(gram, bvec)
        taper = jnp.repeat(loc_level[batch].astype(jnp.float32) / 4.0, BLK)
        anomaly = state - lax.optimization_barrier(jnp.mean(state, axis=0, keepdims=True))
        state = state + taper[None, :] * jnp.dot(mixer.T, anomaly, precision=lax.Precision.HIGHEST)
    return state
```

```python
import functools

import jax
import jax.numpy as jnp
from jax import lax
from jax.experimental import pallas as pl
from jax.experimental.pallas import tpu as pltpu
from jax.sharding import PartitionSpec as P

MESH = pl.DeviceIdType.MESH
F32, BF16, I32 = jnp.float32, jnp.bfloat16, jnp.int32
NBATCH = 2
NSIT = 12
CAP = 24
NX, NZ, NCORE = 4, 8, 2
NY = 8
NXC = NX * NCORE


def split2(x):
    hi = x.astype(BF16)
    lo = (x - hi.astype(F32)).astype(BF16)
    return hi, lo


def split3(x):
    hi = x.astype(BF16)
    rest = x - hi.astype(F32)
    mid = rest.astype(BF16)
    lo = (rest - mid.astype(F32)).astype(BF16)
    return hi, mid, lo


def nn(a, b):
    return lax.dot_general(a, b, (((1,), (0,)), ((), ())), preferred_element_type=F32)


def nt(a, b):
    return lax.dot_general(a, b, (((1,), (1,)), ((), ())), preferred_element_type=F32)


def iota(shape, dim):
    return lax.broadcasted_iota(I32, shape, dim)


def mm(a, b):
    n = a.shape[0]
    ah, al = split2(a)
    bh, bl = split2(b)
    left = jnp.concatenate([ah, al], axis=1)
    row = jnp.concatenate([bh, bl], axis=1)
    both = nn(left, jnp.concatenate([row, row], axis=0))
    return both[:, :n] + both[:, n:]


def wide(a, x):
    ah, al = split2(a)
    xh, xl = split2(x)
    left = jnp.concatenate([ah, al], axis=1)
    return nn(left, jnp.concatenate([xh, xh], axis=0)) + nn(ah, xl)


def ranks(o_row):
    count = o_row.shape[1]
    o_col = jnp.transpose(jnp.broadcast_to(o_row, (128, count)))
    tiles = []
    for t in range(count // 128):
        same = o_col == o_row[:, t * 128 : (t + 1) * 128]
        earlier = iota((count, 128), 0) > iota((count, 128), 1) + t * 128
        tiles.append(jnp.where(same & earlier, 1.0, 0.0).astype(BF16))
    equal = jnp.concatenate(tiles, axis=1)
    rank_col = nn(equal, jnp.ones((count, 128), BF16))
    rank_row = nt(jnp.ones((8, count), BF16), equal)[0:1]
    return o_col, rank_col, rank_row


def compact(grid3, o_col, rank_col, batch, members):
    count = o_col.shape[0]
    o = o_col.astype(I32)
    r = rank_col.astype(I32)
    tile = ((o >> 4) * NCORE + (o & 1)) * NZ + ((o >> 1) & (NZ - 1))
    row = tile * 8 + 3 * batch + (r >> 3)
    rows_all = grid3.shape[0]
    lanes = iota((count, 128), 1)
    onehot = jnp.concatenate(
        [jnp.where(row == lanes + t * 128, 1.0, 0.0).astype(BF16) for t in range(rows_all // 128)],
        axis=1,
    )
    picked = nn(onehot, grid3)
    keep = (lanes >> 4) == (r & 7)
    kept = jnp.concatenate(
        [jnp.where(keep, picked[:, t * 128 : (t + 1) * 128], 0.0).astype(BF16) for t in range(3)],
        axis=1,
    )
    fold = jnp.where((iota((members, 384), 1) & 15) == iota((members, 384), 0), 1.0, 0.0)
    return nt(fold.astype(BF16), kept)


def gauge_taper(levels, o_row, b_row):
    count = o_row.shape[1]
    i = iota((NXC * NZ, count), 0)
    xc, z = i >> 3, i & (NZ - 1)
    owner = ((xc >> 1) * NZ + z) * NCORE + (xc & 1)
    onehot = jnp.where(owner == o_row, 1.0, 0.0).astype(BF16)
    by_block = nn(jnp.transpose(levels).astype(BF16), onehot)
    hit = iota(by_block.shape, 0) == b_row
    return jnp.sum(jnp.where(hit, by_block, 0.0), axis=0, keepdims=True)


def innovations(prior, value, error):
    members = prior.shape[0]
    ymean = jnp.sum(prior, axis=0, keepdims=True) / members
    smat = (prior - ymean) * (1.0 / (error * jnp.sqrt(jnp.float32(members - 1))))
    dvec = (value - ymean) / error
    sh, sl = split2(smat)
    both = jnp.concatenate([sh, sl], axis=0)
    top = nt(sh, both)
    low = nt(sl, both)
    gram = top[:, :members] + (top[:, members:] + low[:, :members]) + low[:, members:]
    bvec = jnp.sum(smat * dvec, axis=1, keepdims=True)
    return gram, bvec


def inverse_root(amat, eye):
    scal = jnp.sum(jnp.sum(amat * eye, axis=1, keepdims=True), axis=0, keepdims=True)

    def newton(_, carry):
        y, z = carry
        q = 1.5 * eye - 0.5 * mm(z, y)
        return mm(y, q), mm(q, z)

    _, z = lax.fori_loop(0, NSIT, newton, (amat / scal, eye))
    return z * lax.rsqrt(scal)


def eliminate(m_ref, amat):
    n = amat.shape[0]
    m_ref[...] = amat
    lane = iota((1, n), 1)
    lanes = iota((n, n), 1)

    def step(index, carry):
        j = 2 * index
        m = m_ref[...]
        r0 = m_ref[pl.ds(j, 1), :]
        r1 = m_ref[pl.ds(j + 1, 1), :]
        at0, at1 = lane == j, lane == j + 1
        a = jnp.sum(jnp.where(at0, r0, 0.0), axis=1, keepdims=True)
        b = jnp.sum(jnp.where(at1, r0, 0.0), axis=1, keepdims=True)
        c = jnp.sum(jnp.where(at1, r1, 0.0), axis=1, keepdims=True)
        c0 = jnp.sum(jnp.where(lanes == j, m, 0.0), axis=1, keepdims=True)
        c1 = jnp.sum(jnp.where(lanes == j + 1, m, 0.0), axis=1, keepdims=True)
        inv_a = 1.0 / a
        ratio = b * inv_a
        inv_d = 1.0 / (c - b * ratio)
        p11 = inv_d
        p01 = -ratio * inv_d
        p00 = inv_a + ratio * ratio * inv_d
        pivot = at0 | at1
        s1 = (r1 - ratio * r0) * inv_d
        u1 = jnp.where(at0, -p01, jnp.where(at1, -p11, s1))
        u0 = jnp.where(at0, -p00, jnp.where(at1, -p01, r0 * inv_a - ratio * s1))
        m_ref[...] = jnp.where((lanes == j) | (lanes == j + 1), 0.0, m) - c0 * u0 - c1 * u1
        m_ref[pl.ds(j, 1), :] = u0
        m_ref[pl.ds(j + 1, 1), :] = u1
        return carry

    lax.fori_loop(0, n // 2, step, 0)


def apply_mix(dmat, wbar, x, taper):
    members = x.shape[0]
    anomaly = x - jnp.sum(x, axis=0, keepdims=True) / members
    shift = jnp.sum(wbar * anomaly, axis=0, keepdims=True) / jnp.sqrt(jnp.float32(members - 1))
    return x + taper * (wide(dmat, anomaly) + shift)


def kernel(
    ens_ref, own_ref, blk_ref, gw_ref, val_ref, err_ref, lvl_ref, out_ref,
    w_ref, b_ref, y_ref, tile_ref, line_ref, grid_ref, prior_ref, full_ref, res_ref, m_ref,
    s1s, s1r, s2s, s2r, s3s, s3r, s4s, s4r, s5s, s5r,
):
    members = ens_ref.shape[0]
    gauges = own_ref.shape[1]
    cell = lax.axis_index("cells")
    my = lax.axis_index("grp")
    core = cell % NCORE
    mz = (cell // NCORE) % NZ
    mx = cell // (NCORE * NZ)
    mxc = mx * NCORE + core

    def z_peer(d):
        return ((mx * NZ + (mz + d) % NZ) * NCORE + core, my)

    def xc_peer(d):
        xc = (mxc + d) % NXC
        return (((xc // NCORE) * NZ + mz) * NCORE + xc % NCORE, my)

    def y_peer(d):
        return (cell, (my + d) % NY)

    barrier = pltpu.get_barrier_semaphore()
    for d in range(1, 8):
        for peer in (z_peer(d), xc_peer(d), y_peer(d)):
            pl.semaphore_signal(barrier, inc=1, device_id=peer, device_id_type=MESH)

    meta = [ranks(own_ref[b : b + 1, :].astype(F32)) for b in range(NBATCH)]
    slot = iota((CAP, gauges), 0)
    for b in range(NBATCH):
        o_row = own_ref[b : b + 1, :]
        mine = (o_row == cell) & (meta[b][2].astype(I32) == slot)
        pick = jnp.where(mine, 1.0, 0.0).astype(BF16)
        g0, g1, g2 = split3(gw_ref[b])
        w_ref[b * CAP : (b + 1) * CAP, :] = nn(pick, g0) + nn(pick, g1) + nn(pick, g2)
        blocks = jnp.broadcast_to(blk_ref[b : b + 1, :], (128, gauges)).astype(F32).astype(BF16)
        b_ref[b * CAP : (b + 1) * CAP, :] = nt(pick, blocks)

    nblk = ens_ref.shape[1] // 128

    def reading(s, carry):
        want = b_ref[pl.ds(s, 1), :]
        got = jnp.zeros((members, 128), F32)
        for k in range(nblk):
            got = jnp.where(want == k, ens_ref[:, k * 128 : (k + 1) * 128], got)
        y_ref[pl.ds(pl.multiple_of(s * members, members), members), :] = got * w_ref[pl.ds(s, 1), :]
        return carry

    lax.fori_loop(0, NBATCH * CAP, reading, 0)
    y3 = jnp.concatenate(split3(y_ref[...]), axis=1)
    flat = nt(jnp.ones((8, y3.shape[1]), BF16), y3)
    sub = iota((8, 128), 0)
    lane = iota((8, 128), 1)
    tile = jnp.zeros((8, 128), F32)
    for r in range(6):
        tile = jnp.where(sub == r, flat[:, r * 128 : (r + 1) * 128], tile)
    for k in range(nblk):
        level = lvl_ref[0, k].astype(F32) * 0.25
        tile = jnp.where((sub == 6) & (lane == k), level, tile)
    tile_ref[...] = tile

    pl.semaphore_wait(barrier, 21)

    def remote(src, dst, send, recv, peer):
        return pltpu.make_async_remote_copy(
            src_ref=src, dst_ref=dst, send_sem=send, recv_sem=recv,
            device_id=peer, device_id_type=MESH,
        )

    chunk = ens_ref.shape[1] // NY

    def rows(y):
        return pl.ds(pl.multiple_of(y * members, members), members)

    def cols(y):
        return pl.ds(pl.multiple_of(y * chunk, chunk), chunk)

    c1 = [
        remote(tile_ref, line_ref.at[mz], s1s.at[d - 1], s1r.at[d - 1], z_peer(d))
        for d in range(1, NZ)
    ]
    for c in c1:
        c.start()
    line_ref[mz] = tile
    c4 = [
        remote(
            ens_ref.at[:, cols((my + d) % NY)], full_ref.at[rows(my)],
            s4s.at[d - 1], s4r.at[d - 1], y_peer(d),
        )
        for d in range(1, NY)
    ]
    for c in c4:
        c.start()
    full_ref[rows(my), :] = ens_ref[:, cols(my)]
    for c in c1:
        c.wait_recv()
    c2 = [
        remote(line_ref, grid_ref.at[mxc], s2s.at[d - 1], s2r.at[d - 1], xc_peer(d))
        for d in range(1, NXC)
    ]
    for c in c2:
        c.start()
    grid_ref[mxc] = line_ref[...]
    for c in c2:
        c.wait_recv()

    grid3 = jnp.concatenate(split3(grid_ref[...].reshape(NXC * NZ * 8, 128)), axis=1)
    c3 = []
    for b in range(NBATCH):
        prior_ref[b, rows(my), :] = compact(grid3, meta[b][0], meta[b][1], b, members)
        c3.append([
            remote(
                prior_ref.at[b, rows(my)], prior_ref.at[b, rows(my)],
                s3s.at[b, d - 1], s3r.at[b, d - 1], y_peer(d),
            )
            for d in range(1, NY)
        ])
        for c in c3[b]:
            c.start()
    levels = grid_ref[:, :, 6, :].reshape(NXC * NZ, 128)
    taper_g = gauge_taper(levels, own_ref[1:2, :], blk_ref[1:2, :])

    def cell_taper(b):
        each = [
            jnp.full((1, 128), lvl_ref[b, my * (chunk // 128) + k].astype(F32) * 0.25, F32)
            for k in range(chunk // 128)
        ]
        return jnp.concatenate(each, axis=1)

    total = members * NY
    eye = jnp.where(iota((total, total), 0) == iota((total, total), 1), 1.0, 0.0)
    for b in range(NBATCH):
        if b == 0:
            for c in c3[0]:
                c.wait_recv()
            prior = prior_ref[0]
        gram, bvec = innovations(prior, val_ref[b : b + 1, :], err_ref[b : b + 1, :])
        amat = eye + gram
        dmat = inverse_root(amat, eye) - eye
        eliminate(m_ref, amat)
        b_row = jnp.sum(eye * bvec, axis=0, keepdims=True)
        wbar = -jnp.sum(m_ref[...] * b_row, axis=1, keepdims=True)
        if b == 0:
            for c in c3[1]:
                c.wait_recv()
            prior = apply_mix(dmat, wbar, prior_ref[1], taper_g)
            for c in c4:
                c.wait_recv()
            state = apply_mix(dmat, wbar, full_ref[...], cell_taper(0))
        else:
            state = apply_mix(dmat, wbar, state, cell_taper(1))
    res_ref[...] = state
    c5 = [
        remote(
            res_ref.at[rows((my + d) % NY)], out_ref.at[:, cols(my)],
            s5s.at[d - 1], s5r.at[d - 1], y_peer(d),
        )
        for d in range(1, NY)
    ]
    for c in c5:
        c.start()
    out_ref[:, cols(my)] = res_ref[rows(my), :]
    for c in c5:
        c.wait_recv()
    for c in c1 + c2 + c3[0] + c3[1] + c4 + c5:
        c.wait_send()


def local(ensemble, gauge_owner, gauge_block, gauge_weight, gauge_value, gauge_error, loc_level):
    members, cells = ensemble.shape
    gauges = gauge_block.shape[1]
    vmem = pl.BlockSpec(memory_space=pltpu.VMEM)
    dma = pltpu.SemaphoreType.DMA
    total = members * NY
    return pl.pallas_call(
        kernel,
        out_shape=jax.ShapeDtypeStruct((members, cells), F32),
        in_specs=[vmem] * 6 + [pl.BlockSpec(memory_space=pltpu.SMEM)],
        out_specs=vmem,
        scratch_shapes=[
            pltpu.VMEM((NBATCH * CAP, 128), F32),
            pltpu.VMEM((NBATCH * CAP, 128), F32),
            pltpu.VMEM((NBATCH * CAP * members, 128), F32),
            pltpu.VMEM((8, 128), F32),
            pltpu.VMEM((NZ, 8, 128), F32),
            pltpu.VMEM((NXC, NZ, 8, 128), F32),
            pltpu.VMEM((NBATCH, total, gauges), F32),
            pltpu.VMEM((total, cells // NY), F32),
            pltpu.VMEM((total, cells // NY), F32),
            pltpu.VMEM((total, total), F32),
            dma((7,)), dma((7,)), dma((7,)), dma((7,)), dma((NBATCH, 7)), dma((NBATCH, 7)),
            dma((7,)), dma((7,)), dma((7,)), dma((7,)),
        ],
        compiler_params=pltpu.CompilerParams(
            collective_id=0, has_side_effects=True, vmem_limit_bytes=48 * 2**20
        ),
    )(
        ensemble, gauge_owner.reshape(NBATCH, gauges), gauge_block, gauge_weight, gauge_value,
        gauge_error, loc_level,
    )


def solution(mesh):
    placed = (P("grp", "cells"), P(), P(), P(), P(), P(), P(None, "cells"))
    return jax.shard_map(
        local, mesh=mesh, in_specs=placed, out_specs=P("grp", "cells"), check_vma=False
    )
```

```python
import functools

import jax
import jax.numpy as jnp
from jax import lax
from jax.experimental import pallas as pl
from jax.experimental.pallas import tpu as pltpu
from jax.sharding import PartitionSpec as P

MESH = pl.DeviceIdType.MESH
F32, BF16, I32 = jnp.float32, jnp.bfloat16, jnp.int32
NBATCH = 2
NSIT = 12
CAP = 24
PIVOTS = 4
NX, NZ, NCORE = 4, 8, 2
NY = 8
NXC = NX * NCORE
FAR_FIRST = (4, 3, 5, 2, 6, 1, 7)


def split2(x):
    hi = x.astype(BF16)
    lo = (x - hi.astype(F32)).astype(BF16)
    return hi, lo


def split3(x):
    hi = x.astype(BF16)
    rest = x - hi.astype(F32)
    mid = rest.astype(BF16)
    lo = (rest - mid.astype(F32)).astype(BF16)
    return hi, mid, lo


def nn(a, b):
    return lax.dot_general(a, b, (((1,), (0,)), ((), ())), preferred_element_type=F32)


def nt(a, b):
    return lax.dot_general(a, b, (((1,), (1,)), ((), ())), preferred_element_type=F32)


def iota(shape, dim):
    return lax.broadcasted_iota(I32, shape, dim)


def wide(a, x):
    ah, al = split2(a)
    xh, xl = split2(x)
    left = jnp.concatenate([ah, al], axis=1)
    return nn(left, jnp.concatenate([xh, xh], axis=0)) + nn(ah, xl)


def ranks(o_row):
    count = o_row.shape[1]
    o_col = jnp.transpose(jnp.broadcast_to(o_row, (128, count)))
    tiles = []
    for t in range(count // 128):
        same = o_col == o_row[:, t * 128 : (t + 1) * 128]
        earlier = iota((count, 128), 0) > iota((count, 128), 1) + t * 128
        tiles.append(jnp.where(same & earlier, 1.0, 0.0).astype(BF16))
    equal = jnp.concatenate(tiles, axis=1)
    rank_col = nn(equal, jnp.ones((count, 128), BF16))
    rank_row = nt(jnp.ones((8, count), BF16), equal)[0:1]
    return o_col, rank_col, rank_row


def places(o_col, rank_col):
    o = o_col.astype(I32)
    r = rank_col.astype(I32)
    tile = ((o >> 4) * NCORE + (o & 1)) * NZ + ((o >> 1) & (NZ - 1))
    return (r >> 3) * (NXC * NZ) + tile, r & 7


def compact(grid3, row, group, members):
    count = row.shape[0]
    lanes = iota((count, 128), 1)
    onehot = jnp.concatenate(
        [
            jnp.where(row == lanes + t * 128, 1.0, 0.0).astype(BF16)
            for t in range(pl.cdiv(grid3.shape[0], 128))
        ],
        axis=1,
    )[:, : grid3.shape[0]]
    picked = nn(onehot, grid3)
    keep = (lanes >> 4) == group
    kept = jnp.concatenate(
        [jnp.where(keep, picked[:, t * 128 : (t + 1) * 128], 0.0).astype(BF16) for t in range(3)],
        axis=1,
    )
    fold = jnp.where((iota((members, 384), 1) & 15) == iota((members, 384), 0), 1.0, 0.0)
    return nt(fold.astype(BF16), kept)


def gauge_taper(levels, o_row, b_row):
    count = o_row.shape[1]
    i = iota((NXC * NZ, count), 0)
    xc, z = i >> 3, i & (NZ - 1)
    owner = ((xc >> 1) * NZ + z) * NCORE + (xc & 1)
    onehot = jnp.where(owner == o_row, 1.0, 0.0).astype(BF16)
    by_block = nn(jnp.transpose(levels).astype(BF16), onehot)
    hit = iota(by_block.shape, 0) == b_row
    return jnp.sum(jnp.where(hit, by_block, 0.0), axis=0, keepdims=True)


def innovations(prior, value, error):
    members = prior.shape[0]
    ymean = jnp.sum(prior, axis=0, keepdims=True) / members
    smat = (prior - ymean) * (1.0 / (error * jnp.sqrt(jnp.float32(members - 1))))
    dvec = (value - ymean) / error
    sh, sl = split2(smat)
    both = jnp.concatenate([sh, sl], axis=0)
    top = nt(sh, both)
    low = nt(sl, both)
    gram = top[:, :members] + (top[:, members:] + low[:, :members]) + low[:, members:]
    bvec = jnp.sum(smat * dvec, axis=1, keepdims=True)
    return gram, bvec


def stacked(x):
    hi, lo = split2(x)
    row = jnp.concatenate([hi, lo], axis=1)
    return jnp.concatenate([row, row], axis=0)


def halves(x):
    return jnp.concatenate(split2(x), axis=1)


def joined(x):
    n = x.shape[1] // 2
    return x[:, :n] + x[:, n:]


def newton(eye, y, z):
    wy, wz = stacked(y), stacked(z)
    q = 1.5 * eye - 0.5 * joined(nn(halves(z), wy))
    hq = halves(q)
    return joined(nn(hq, wy)), joined(nn(hq, wz))


def sweep(m_ref, j):
    n = m_ref.shape[0]
    span = range(PIVOTS)
    lane = iota((1, n), 1)
    m = m_ref[...]
    rows = [m_ref[pl.ds(j + i, 1), :] for i in span]
    at = [lane == j + i for i in span]
    e = [[None] * PIVOTS for _ in span]
    for i in span:
        for k in range(i, PIVOTS):
            e[i][k] = e[k][i] = jnp.sum(jnp.where(at[k], rows[i], 0.0), axis=1, keepdims=True)
    cols = [jnp.sum(jnp.where(at[k], m, 0.0), axis=1, keepdims=True) for k in span]
    for q in span:
        inv = 1.0 / e[q][q]
        scaled = [e[q][k] * inv for k in span]
        new = [[None] * PIVOTS for _ in span]
        for i in span:
            for k in range(i, PIVOTS):
                if i == q and k == q:
                    v = -inv
                elif i == q or k == q:
                    v = scaled[k if i == q else i]
                else:
                    v = e[i][k] - e[i][q] * scaled[k]
                new[i][k] = new[k][i] = v
        e = new
    u = []
    for i in span:
        acc = -e[i][0] * rows[0]
        for k in range(1, PIVOTS):
            acc = acc - e[i][k] * rows[k]
        for k in span:
            acc = jnp.where(at[k], e[i][k], acc)
        u.append(acc)
    pivot = functools.reduce(jnp.logical_or, at)
    new = jnp.where(pivot, 0.0, m)
    for i in span:
        new = new - cols[i] * u[i]
    m_ref[...] = new
    for i in span:
        m_ref[pl.ds(j + i, 1), :] = u[i]


def transform(m_ref, amat, eye, between):
    scal = jnp.sum(jnp.sum(amat * eye, axis=1, keepdims=True), axis=0, keepdims=True)
    m_ref[...] = amat
    steps = amat.shape[0] // PIVOTS
    most = NSIT - 2

    def three(i, carry):
        for k in range(3):
            sweep(m_ref, (i * 3 + k) * PIVOTS)
        return newton(eye, *carry)

    def one(i, carry):
        sweep(m_ref, (steps - NSIT + i) * PIVOTS)
        return newton(eye, *carry)

    carry = lax.fori_loop(0, most, three, (amat / scal, eye))
    between()
    _, z = lax.fori_loop(most, NSIT, one, carry)
    return z * lax.rsqrt(scal)


def apply_mix(dmat, wbar, x, taper):
    members = x.shape[0]
    anomaly = x - jnp.sum(x, axis=0, keepdims=True) / members
    shift = jnp.sum(wbar * anomaly, axis=0, keepdims=True) / jnp.sqrt(jnp.float32(members - 1))
    return x + taper * (wide(dmat, anomaly) + shift)


def kernel(
    ens_hbm, own_hbm, blk_hbm, gw_hbm, val_hbm, err_hbm, lvl_hbm, out_ref,
    ens_ref, own_ref, blk_ref, gw_ref, val_ref, err_ref, lvl_ref, cps,
    w_ref, b_ref, y_ref, row_ref, group_ref, tile_ref, line_ref, grid_ref, prior_ref, full_ref,
    res_ref, m_ref, s1s, s1r, s2s, s2r, s3s, s3r, s4s, s4r, s5s, s5r, s6s, s6r,
):
    members = ens_ref.shape[0]
    gauges = blk_ref.shape[1]
    half = gauges // NCORE
    cell = lax.axis_index("cells")
    my = lax.axis_index("grp")
    core = cell % NCORE
    mz = (cell // NCORE) % NZ
    mx = cell // (NCORE * NZ)
    mxc = mx * NCORE + core

    def z_peer(d):
        return ((mx * NZ + (mz + d) % NZ) * NCORE + core, my)

    def xc_peer(d):
        xc = (mxc + d) % NXC
        return (((xc // NCORE) * NZ + mz) * NCORE + xc % NCORE, my)

    def y_peer(d):
        return (cell, (my + d) % NY)

    twin = (cell + 1 - 2 * core, my)

    barrier = pltpu.get_barrier_semaphore()
    for d in FAR_FIRST:
        for peer in (z_peer(d), xc_peer(d), y_peer(d)):
            pl.semaphore_signal(barrier, inc=1, device_id=peer, device_id_type=MESH)

    pairs = [
        (own_hbm, own_ref), (blk_hbm, blk_ref), (gw_hbm, gw_ref), (lvl_hbm, lvl_ref),
        (ens_hbm, ens_ref), (val_hbm, val_ref), (err_hbm, err_ref),
    ]
    staged = [pltpu.make_async_copy(a, b, cps.at[i]) for i, (a, b) in enumerate(pairs)]
    for c in staged:
        c.start()
    for c in staged[:3]:
        c.wait()

    slot = iota((CAP, gauges), 0)
    for b in range(NBATCH):
        o_row = own_ref[b]
        o_col, rank_col, rank_row = ranks(o_row.astype(F32))
        row_ref[b], group_ref[b] = places(o_col, rank_col)
        mine = (o_row == cell) & (rank_row.astype(I32) == slot)
        pick = jnp.where(mine, 1.0, 0.0).astype(BF16)
        g0, g1, g2 = split3(gw_ref[b])
        w_ref[b * CAP : (b + 1) * CAP, :] = nn(pick, g0) + nn(pick, g1) + nn(pick, g2)
        blocks = jnp.broadcast_to(blk_ref[b : b + 1, :], (128, gauges)).astype(F32).astype(BF16)
        b_ref[b * CAP : (b + 1) * CAP, :] = nt(pick, blocks)

    for c in staged[3:]:
        c.wait()
    nblk = ens_ref.shape[1] // 128

    def reading(s, carry):
        want = b_ref[pl.ds(s, 1), :]
        got = jnp.zeros((members, 128), F32)
        for k in range(nblk):
            got = jnp.where(want == k, ens_ref[:, k * 128 : (k + 1) * 128], got)
        y_ref[pl.ds(pl.multiple_of(s * members, members), members), :] = got * w_ref[pl.ds(s, 1), :]
        return carry

    lax.fori_loop(0, NBATCH * CAP, reading, 0)
    y3 = jnp.concatenate(split3(y_ref[...]), axis=1)
    flat = nt(jnp.ones((8, y3.shape[1]), BF16), y3)[:4]
    sub = iota((4, 128), 0)
    lane = iota((4, 128), 1)
    for b in range(NBATCH):
        tile = jnp.zeros((4, 128), F32)
        for r in range(3):
            tile = jnp.where(sub == r, flat[:, (3 * b + r) * 128 : (3 * b + r + 1) * 128], tile)
        if b == 0:
            for k in range(nblk):
                level = lvl_ref[0, k].astype(F32) * 0.25
                tile = jnp.where((sub == 3) & (lane == k), level, tile)
        tile_ref[b] = tile

    pl.semaphore_wait(barrier, 21)

    def remote(src, dst, send, recv, peer):
        return pltpu.make_async_remote_copy(
            src_ref=src, dst_ref=dst, send_sem=send, recv_sem=recv,
            device_id=peer, device_id_type=MESH,
        )

    chunk = ens_ref.shape[1] // NY

    def rows(y):
        return pl.ds(pl.multiple_of(y * members, members), members)

    def cols(y):
        return pl.ds(pl.multiple_of(y * chunk, chunk), chunk)

    c1 = [
        remote(tile_ref, line_ref.at[:, mz], s1s.at[d - 1], s1r.at[d - 1], z_peer(d))
        for d in FAR_FIRST
    ]
    for c in c1:
        c.start()
    for b in range(NBATCH):
        line_ref[b, mz] = tile_ref[b]
    c4 = [
        remote(
            ens_ref.at[:, cols((my + d) % NY)], full_ref.at[rows(my)],
            s4s.at[d - 1], s4r.at[d - 1], y_peer(d),
        )
        for d in FAR_FIRST
    ]
    for c in c4:
        c.start()
    full_ref[rows(my), :] = ens_ref[:, cols(my)]
    for c in c1:
        c.wait_recv()
    c2 = [
        [
            remote(
                line_ref.at[b], grid_ref.at[b, mxc], s2s.at[b, d - 1], s2r.at[b, d - 1], xc_peer(d)
            )
            for d in FAR_FIRST
        ]
        for b in range(NBATCH)
    ]
    c3 = [
        [
            remote(
                prior_ref.at[b, core, rows(my)], prior_ref.at[b, core, rows(my)],
                s3s.at[b, d - 1], s3r.at[b, d - 1], y_peer(d),
            )
            for d in FAR_FIRST
        ]
        for b in range(NBATCH)
    ]
    c6 = [
        [
            remote(
                prior_ref.at[b, core, rows((my + NY - d) % NY)],
                prior_ref.at[b, core, rows((my + NY - d) % NY)],
                s6s.at[b, d], s6r.at[b, d], twin,
            )
            for d in (0,) + FAR_FIRST
        ]
        for b in range(NBATCH)
    ]

    def packed(b):
        parts = [grid_ref[b, :, :, r, :].reshape(NXC * NZ, 128) for r in range(3)]
        grid3 = jnp.concatenate(split3(jnp.concatenate(parts, axis=0)), axis=1)
        mine = pl.ds(pl.multiple_of(core * half, half), half)
        prior_ref[b, core, rows(my), :] = compact(
            grid3, row_ref[b, mine, :], group_ref[b, mine, :], members
        )

    def onward(b):
        for c, f in zip(c3[b][::-1], c6[b][:0:-1]):
            c.wait_recv()
            f.start()

    for b in range(NBATCH):
        for c in c2[b]:
            c.start()
        grid_ref[b, mxc] = line_ref[b]
    for c in c2[0]:
        c.wait_recv()
    packed(0)
    for c in c3[0] + c6[0][:1]:
        c.start()
    for c in c2[1]:
        c.wait_recv()
    packed(1)
    levels = grid_ref[0, :, :, 3, :].reshape(NXC * NZ, 128)
    taper_g = gauge_taper(levels, own_ref[1], blk_ref[1:2, :])
    onward(0)
    for c in c3[1] + c6[1][:1]:
        c.start()
    for c in c6[0]:
        c.wait_recv()

    def cell_taper(b):
        each = [
            jnp.full((1, 128), lvl_ref[b, my * (chunk // 128) + k].astype(F32) * 0.25, F32)
            for k in range(chunk // 128)
        ]
        return jnp.concatenate(each, axis=1)

    def prior_of(b):
        return jnp.concatenate([prior_ref[b, h] for h in range(NCORE)], axis=1)

    total = members * NY
    eye = jnp.where(iota((total, total), 0) == iota((total, total), 1), 1.0, 0.0)
    prior = prior_of(0)
    for b in range(NBATCH):
        gram, bvec = innovations(prior, val_ref[b : b + 1, :], err_ref[b : b + 1, :])
        amat = eye + gram
        between = functools.partial(onward, 1) if b == 0 else lambda: None
        dmat = transform(m_ref, amat, eye, between) - eye
        b_row = jnp.sum(eye * bvec, axis=0, keepdims=True)
        wbar = -jnp.sum(m_ref[...] * b_row, axis=1, keepdims=True)
        if b == 0:
            for c in c6[1]:
                c.wait_recv()
            prior = apply_mix(dmat, wbar, prior_of(1), taper_g)
            for c in c4:
                c.wait_recv()
            state = apply_mix(dmat, wbar, full_ref[...], cell_taper(0))
        else:
            state = apply_mix(dmat, wbar, state, cell_taper(1))
    res_ref[...] = state
    c5 = [
        remote(
            res_ref.at[rows((my + d) % NY)], out_ref.at[:, cols(my)],
            s5s.at[d - 1], s5r.at[d - 1], y_peer(d),
        )
        for d in FAR_FIRST
    ]
    for c in c5:
        c.start()
    out_ref[:, cols(my)] = res_ref[rows(my), :]
    for c in c5:
        c.wait_recv()
    for c in c1 + c2[0] + c2[1] + c3[0] + c3[1] + c4 + c5 + c6[0] + c6[1]:
        c.wait_send()


def local(ensemble, gauge_owner, gauge_block, gauge_weight, gauge_value, gauge_error, loc_level):
    members, cells = ensemble.shape
    gauges = gauge_block.shape[1]
    vmem = pl.BlockSpec(memory_space=pltpu.VMEM)
    hbm = pl.BlockSpec(memory_space=pltpu.HBM)
    dma = pltpu.SemaphoreType.DMA
    total = members * NY
    operands = (
        ensemble, jnp.swapaxes(gauge_owner, 1, 2), gauge_block, gauge_weight, gauge_value,
        gauge_error, loc_level,
    )
    staged = [pltpu.VMEM(a.shape, a.dtype) for a in operands[:-1]]
    return pl.pallas_call(
        kernel,
        out_shape=jax.ShapeDtypeStruct((members, cells), F32),
        in_specs=[hbm] * 7,
        out_specs=vmem,
        scratch_shapes=staged + [
            pltpu.SMEM(loc_level.shape, I32),
            dma((7,)),
            pltpu.VMEM((NBATCH * CAP, 128), F32),
            pltpu.VMEM((NBATCH * CAP, 128), F32),
            pltpu.VMEM((NBATCH * CAP * members, 128), F32),
            pltpu.VMEM((NBATCH, gauges, 128), I32),
            pltpu.VMEM((NBATCH, gauges, 128), I32),
            pltpu.VMEM((NBATCH, 4, 128), F32),
            pltpu.VMEM((NBATCH, NZ, 4, 128), F32),
            pltpu.VMEM((NBATCH, NXC, NZ, 4, 128), F32),
            pltpu.VMEM((NBATCH, NCORE, total, gauges // NCORE), F32),
            pltpu.VMEM((total, cells // NY), F32),
            pltpu.VMEM((total, cells // NY), F32),
            pltpu.VMEM((total, total), F32),
            dma((7,)), dma((7,)), dma((NBATCH, 7)), dma((NBATCH, 7)), dma((NBATCH, 7)),
            dma((NBATCH, 7)), dma((7,)), dma((7,)), dma((7,)), dma((7,)),
            dma((NBATCH, 8)), dma((NBATCH, 8)),
        ],
        compiler_params=pltpu.CompilerParams(
            collective_id=0, has_side_effects=True, vmem_limit_bytes=63 * 2**20
        ),
    )(*operands)


def solution(mesh):
    placed = (P("grp", "cells"), P(), P(), P(), P(), P(), P(None, "cells"))
    return jax.shard_map(
        local, mesh=mesh, in_specs=placed, out_specs=P("grp", "cells"), check_vma=False
    )
```

```python
import functools

import jax
import jax.numpy as jnp
from jax import lax
from jax.experimental import pallas as pl
from jax.experimental.pallas import tpu as pltpu
from jax.sharding import PartitionSpec as P

MESH = pl.DeviceIdType.MESH
F32, BF16, I32 = jnp.float32, jnp.bfloat16, jnp.int32
NBATCH = 2
NSIT = 12
CAP = 24
PIVOTS = 4
NX, NZ, NCORE = 4, 8, 2
NY = 8
NXC = NX * NCORE
FAR_FIRST = (4, 3, 5, 2, 6, 1, 7)


def split2(x):
    hi = x.astype(BF16)
    lo = (x - hi.astype(F32)).astype(BF16)
    return hi, lo


def split3(x):
    hi = x.astype(BF16)
    rest = x - hi.astype(F32)
    mid = rest.astype(BF16)
    lo = (rest - mid.astype(F32)).astype(BF16)
    return hi, mid, lo


def nn(a, b):
    return lax.dot_general(a, b, (((1,), (0,)), ((), ())), preferred_element_type=F32)


def nt(a, b):
    return lax.dot_general(a, b, (((1,), (1,)), ((), ())), preferred_element_type=F32)


def iota(shape, dim):
    return lax.broadcasted_iota(I32, shape, dim)


def wide(a, x):
    ah, al = split2(a)
    xh, xl = split2(x)
    left = jnp.concatenate([ah, al], axis=1)
    return nn(left, jnp.concatenate([xh, xh], axis=0)) + nn(ah, xl)


def ranks(o_row):
    count = o_row.shape[1]
    o_col = jnp.transpose(jnp.broadcast_to(o_row, (128, count)))
    tiles = []
    for t in range(count // 128):
        same = o_col == o_row[:, t * 128 : (t + 1) * 128]
        earlier = iota((count, 128), 0) > iota((count, 128), 1) + t * 128
        tiles.append(jnp.where(same & earlier, 1.0, 0.0).astype(BF16))
    equal = jnp.concatenate(tiles, axis=1)
    rank_col = nn(equal, jnp.ones((count, 128), BF16))
    rank_row = nt(jnp.ones((8, count), BF16), equal)[0:1]
    return o_col, rank_col, rank_row


def places(o_col, rank_col):
    o = o_col.astype(I32)
    r = rank_col.astype(I32)
    tile = ((o >> 4) * NCORE + (o & 1)) * NZ + ((o >> 1) & (NZ - 1))
    return (r >> 3) * (NXC * NZ) + tile, r & 7


def compact(grid3, row, group, members):
    count = row.shape[0]
    lanes = iota((count, 128), 1)
    onehot = jnp.concatenate(
        [
            jnp.where(row == lanes + t * 128, 1.0, 0.0).astype(BF16)
            for t in range(pl.cdiv(grid3.shape[0], 128))
        ],
        axis=1,
    )[:, : grid3.shape[0]]
    picked = nn(onehot, grid3)
    keep = (lanes >> 4) == group
    kept = jnp.concatenate(
        [jnp.where(keep, picked[:, t * 128 : (t + 1) * 128], 0.0).astype(BF16) for t in range(3)],
        axis=1,
    )
    fold = jnp.where((iota((members, 384), 1) & 15) == iota((members, 384), 0), 1.0, 0.0)
    return nt(fold.astype(BF16), kept)


def gauge_taper(levels, o_row, b_row):
    count = o_row.shape[1]
    i = iota((NXC * NZ, count), 0)
    xc, z = i >> 3, i & (NZ - 1)
    owner = ((xc >> 1) * NZ + z) * NCORE + (xc & 1)
    onehot = jnp.where(owner == o_row, 1.0, 0.0).astype(BF16)
    by_block = nn(jnp.transpose(levels).astype(BF16), onehot)
    hit = iota(by_block.shape, 0) == b_row
    return jnp.sum(jnp.where(hit, by_block, 0.0), axis=0, keepdims=True)


def innovations(prior, value, error):
    members = prior.shape[0]
    ymean = jnp.sum(prior, axis=0, keepdims=True) / members
    smat = (prior - ymean) * (1.0 / (error * jnp.sqrt(jnp.float32(members - 1))))
    dvec = (value - ymean) / error
    sh, sl = split2(smat)
    both = jnp.concatenate([sh, sl], axis=0)
    top = nt(sh, both)
    low = nt(sl, both)
    gram = top[:, :members] + (top[:, members:] + low[:, :members]) + low[:, members:]
    bvec = jnp.sum(smat * dvec, axis=1, keepdims=True)
    return gram, bvec


def stacked(x):
    hi, lo = split2(x)
    row = jnp.concatenate([hi, lo], axis=1)
    return jnp.concatenate([row, row], axis=0)


def halves(x):
    return jnp.concatenate(split2(x), axis=1)


def joined(x):
    n = x.shape[1] // 2
    return x[:, :n] + x[:, n:]


def newton(eye, y, z):
    wy, wz = stacked(y), stacked(z)
    q = 1.5 * eye - 0.5 * joined(nn(halves(z), wy))
    hq = halves(q)
    return joined(nn(hq, wy)), joined(nn(hq, wz))


def sweep(m_ref, j):
    n = m_ref.shape[0]
    span = range(PIVOTS)
    lane = iota((1, n), 1)
    m = m_ref[...]
    rows = [m_ref[pl.ds(j + i, 1), :] for i in span]
    at = [lane == j + i for i in span]
    e = [[None] * PIVOTS for _ in span]
    for i in span:
        for k in range(i, PIVOTS):
            e[i][k] = e[k][i] = jnp.sum(jnp.where(at[k], rows[i], 0.0), axis=1, keepdims=True)
    cols = [jnp.sum(jnp.where(at[k], m, 0.0), axis=1, keepdims=True) for k in span]
    for q in span:
        inv = 1.0 / e[q][q]
        scaled = [e[q][k] * inv for k in span]
        new = [[None] * PIVOTS for _ in span]
        for i in span:
            for k in range(i, PIVOTS):
                if i == q and k == q:
                    v = -inv
                elif i == q or k == q:
                    v = scaled[k if i == q else i]
                else:
                    v = e[i][k] - e[i][q] * scaled[k]
                new[i][k] = new[k][i] = v
        e = new
    u = []
    for i in span:
        acc = -e[i][0] * rows[0]
        for k in range(1, PIVOTS):
            acc = acc - e[i][k] * rows[k]
        for k in span:
            acc = jnp.where(at[k], e[i][k], acc)
        u.append(acc)
    pivot = functools.reduce(jnp.logical_or, at)
    new = jnp.where(pivot, 0.0, m)
    for i in span:
        new = new - cols[i] * u[i]
    m_ref[...] = new
    for i in span:
        m_ref[pl.ds(j + i, 1), :] = u[i]


def transform(m_ref, amat, eye, between):
    scal = jnp.sum(jnp.sum(amat * eye, axis=1, keepdims=True), axis=0, keepdims=True)
    m_ref[...] = amat
    steps = amat.shape[0] // PIVOTS
    most = NSIT - 2

    def three(i, carry):
        for k in range(3):
            sweep(m_ref, (i * 3 + k) * PIVOTS)
        return newton(eye, *carry)

    def one(i, carry):
        sweep(m_ref, (steps - NSIT + i) * PIVOTS)
        return newton(eye, *carry)

    carry = lax.fori_loop(0, most, three, (amat / scal, eye))
    between()
    _, z = lax.fori_loop(most, NSIT, one, carry)
    return z * lax.rsqrt(scal)


def apply_mix(dmat, wbar, x, taper):
    members = x.shape[0]
    anomaly = x - jnp.sum(x, axis=0, keepdims=True) / members
    shift = jnp.sum(wbar * anomaly, axis=0, keepdims=True) / jnp.sqrt(jnp.float32(members - 1))
    return x + taper * (wide(dmat, anomaly) + shift)


def kernel(
    ens_hbm, own_hbm, blk_hbm, gw_hbm, val_hbm, err_hbm, lvl_hbm, out_ref,
    ens_ref, own_ref, blk_ref, gw_ref, val_ref, err_ref, lvl_ref, cps,
    w_ref, b_ref, y_ref, row_ref, group_ref, tile_ref, line_ref, grid_ref, prior_ref, full_ref,
    res_ref, m_ref, s1s, s1r, s2s, s2r, s3s, s3r, s4s, s4r, s5s, s5r, s6s, s6r,
):
    members = ens_ref.shape[0]
    gauges = blk_ref.shape[1]
    half = gauges // NCORE
    cell = lax.axis_index("cells")
    my = lax.axis_index("grp")
    core = cell % NCORE
    mz = (cell // NCORE) % NZ
    mx = cell // (NCORE * NZ)
    mxc = mx * NCORE + core

    def z_peer(d):
        return ((mx * NZ + (mz + d) % NZ) * NCORE + core, my)

    def xc_peer(d):
        xc = (mxc + d) % NXC
        return (((xc // NCORE) * NZ + mz) * NCORE + xc % NCORE, my)

    def y_peer(d):
        return (cell, (my + d) % NY)

    twin = (cell + 1 - 2 * core, my)

    barrier = pltpu.get_barrier_semaphore()
    for d in FAR_FIRST:
        for peer in (z_peer(d), xc_peer(d), y_peer(d)):
            pl.semaphore_signal(barrier, inc=1, device_id=peer, device_id_type=MESH)

    pairs = [
        (own_hbm, own_ref), (blk_hbm, blk_ref), (gw_hbm.at[0], gw_ref.at[0]), (ens_hbm, ens_ref),
        (lvl_hbm, lvl_ref), (gw_hbm.at[1], gw_ref.at[1]), (val_hbm, val_ref), (err_hbm, err_ref),
    ]
    staged = [pltpu.make_async_copy(a, b, cps.at[i]) for i, (a, b) in enumerate(pairs)]
    for c in staged:
        c.start()
    nblk = ens_ref.shape[1] // 128

    def readings(b):
        slot = iota((CAP, gauges), 0)
        o_row = own_ref[b]
        o_col, rank_col, rank_row = ranks(o_row.astype(F32))
        row_ref[b], group_ref[b] = places(o_col, rank_col)
        mine = (o_row == cell) & (rank_row.astype(I32) == slot)
        pick = jnp.where(mine, 1.0, 0.0).astype(BF16)
        g0, g1, g2 = split3(gw_ref[b])
        w_ref[...] = nn(pick, g0) + nn(pick, g1) + nn(pick, g2)
        blocks = jnp.broadcast_to(blk_ref[b : b + 1, :], (128, gauges)).astype(F32).astype(BF16)
        b_ref[...] = nt(pick, blocks)
        if b == 0:
            staged[3].wait()

        def reading(s, carry):
            want = b_ref[pl.ds(s, 1), :]
            got = jnp.zeros((members, 128), F32)
            for k in range(nblk):
                got = jnp.where(want == k, ens_ref[:, k * 128 : (k + 1) * 128], got)
            at = pl.ds(pl.multiple_of(s * members, members), members)
            y_ref[at, :] = got * w_ref[pl.ds(s, 1), :]
            return carry

        lax.fori_loop(0, CAP, reading, 0, unroll=4)
        y3 = jnp.concatenate(split3(y_ref[...]), axis=1)
        flat = nt(jnp.ones((8, y3.shape[1]), BF16), y3)[:4]
        sub = iota((4, 128), 0)
        lane = iota((4, 128), 1)
        tile = jnp.zeros((4, 128), F32)
        for r in range(3):
            tile = jnp.where(sub == r, flat[:, r * 128 : (r + 1) * 128], tile)
        if b == 1:
            for k in range(nblk):
                level = lvl_ref[0, k].astype(F32) * 0.25
                tile = jnp.where((sub == 3) & (lane == k), level, tile)
        tile_ref[b] = tile

    for c in staged[:3]:
        c.wait()
    readings(0)
    for c in staged[4:]:
        c.wait()

    pl.semaphore_wait(barrier, 21)

    def remote(src, dst, send, recv, peer):
        return pltpu.make_async_remote_copy(
            src_ref=src, dst_ref=dst, send_sem=send, recv_sem=recv,
            device_id=peer, device_id_type=MESH,
        )

    chunk = ens_ref.shape[1] // NY

    def rows(y):
        return pl.ds(pl.multiple_of(y * members, members), members)

    def cols(y):
        return pl.ds(pl.multiple_of(y * chunk, chunk), chunk)

    c1 = [
        [
            remote(
                tile_ref.at[b], line_ref.at[b, mz], s1s.at[b, d - 1], s1r.at[b, d - 1], z_peer(d)
            )
            for d in FAR_FIRST
        ]
        for b in range(NBATCH)
    ]
    c4 = [
        remote(
            ens_ref.at[:, cols((my + d) % NY)], full_ref.at[rows(my)],
            s4s.at[d - 1], s4r.at[d - 1], y_peer(d),
        )
        for d in FAR_FIRST
    ]
    for c in c1[0] + c4:
        c.start()
    readings(1)
    for c in c1[1]:
        c.start()
    full_ref[rows(my), :] = ens_ref[:, cols(my)]
    for b in range(NBATCH):
        line_ref[b, mz] = tile_ref[b]
    c2 = [
        [
            remote(
                line_ref.at[b], grid_ref.at[b, mxc], s2s.at[b, d - 1], s2r.at[b, d - 1], xc_peer(d)
            )
            for d in FAR_FIRST
        ]
        for b in range(NBATCH)
    ]
    c3 = [
        [
            remote(
                prior_ref.at[b, core, rows(my)], prior_ref.at[b, core, rows(my)],
                s3s.at[b, d - 1], s3r.at[b, d - 1], y_peer(d),
            )
            for d in FAR_FIRST
        ]
        for b in range(NBATCH)
    ]
    c6 = [
        [
            remote(
                prior_ref.at[b, core, rows((my + NY - d) % NY)],
                prior_ref.at[b, core, rows((my + NY - d) % NY)],
                s6s.at[b, d], s6r.at[b, d], twin,
            )
            for d in (0,) + FAR_FIRST
        ]
        for b in range(NBATCH)
    ]

    def packed(b):
        parts = [grid_ref[b, :, :, r, :].reshape(NXC * NZ, 128) for r in range(3)]
        grid3 = jnp.concatenate(split3(jnp.concatenate(parts, axis=0)), axis=1)
        mine = pl.ds(pl.multiple_of(core * half, half), half)
        prior_ref[b, core, rows(my), :] = compact(
            grid3, row_ref[b, mine, :], group_ref[b, mine, :], members
        )

    def onward(b):
        for c, f in zip(c3[b][::-1], c6[b][:0:-1]):
            c.wait_recv()
            f.start()

    for b in range(NBATCH):
        for c in c1[b]:
            c.wait_recv()
        for c in c2[b]:
            c.start()
        grid_ref[b, mxc] = line_ref[b]
    for c in c2[0]:
        c.wait_recv()
    packed(0)
    for c in c3[0] + c6[0][:1]:
        c.start()
    for c in c2[1]:
        c.wait_recv()
    packed(1)
    levels = grid_ref[1, :, :, 3, :].reshape(NXC * NZ, 128)
    taper_g = gauge_taper(levels, own_ref[1], blk_ref[1:2, :])
    onward(0)
    for c in c3[1] + c6[1][:1]:
        c.start()
    for c in c6[0] + c4:
        c.wait_recv()

    def cell_taper(b):
        each = [
            jnp.full((1, 128), lvl_ref[b, my * (chunk // 128) + k].astype(F32) * 0.25, F32)
            for k in range(chunk // 128)
        ]
        return jnp.concatenate(each, axis=1)

    def prior_of(b):
        return jnp.concatenate([prior_ref[b, h] for h in range(NCORE)], axis=1)

    total = members * NY
    eye = jnp.where(iota((total, total), 0) == iota((total, total), 1), 1.0, 0.0)
    prior = prior_of(0)
    for b in range(NBATCH):
        gram, bvec = innovations(prior, val_ref[b : b + 1, :], err_ref[b : b + 1, :])
        amat = eye + gram
        between = functools.partial(onward, 1) if b == 0 else lambda: None
        dmat = transform(m_ref, amat, eye, between) - eye
        b_row = jnp.sum(eye * bvec, axis=0, keepdims=True)
        wbar = -jnp.sum(m_ref[...] * b_row, axis=1, keepdims=True)
        if b == 0:
            for c in c6[1]:
                c.wait_recv()
            prior = apply_mix(dmat, wbar, prior_of(1), taper_g)
            state = apply_mix(dmat, wbar, full_ref[...], cell_taper(0))
        else:
            state = apply_mix(dmat, wbar, state, cell_taper(1))
    res_ref[...] = state
    c5 = [
        remote(
            res_ref.at[rows((my + d) % NY)], out_ref.at[:, cols(my)],
            s5s.at[d - 1], s5r.at[d - 1], y_peer(d),
        )
        for d in FAR_FIRST
    ]
    for c in c5:
        c.start()
    out_ref[:, cols(my)] = res_ref[rows(my), :]
    for c in c5:
        c.wait_recv()
    for c in c1[0] + c1[1] + c2[0] + c2[1] + c3[0] + c3[1] + c4 + c5 + c6[0] + c6[1]:
        c.wait_send()


def local(ensemble, gauge_owner, gauge_block, gauge_weight, gauge_value, gauge_error, loc_level):
    members, cells = ensemble.shape
    gauges = gauge_block.shape[1]
    vmem = pl.BlockSpec(memory_space=pltpu.VMEM)
    hbm = pl.BlockSpec(memory_space=pltpu.HBM)
    dma = pltpu.SemaphoreType.DMA
    total = members * NY
    operands = (
        ensemble, jnp.swapaxes(gauge_owner, 1, 2), gauge_block, gauge_weight, gauge_value,
        gauge_error, loc_level,
    )
    staged = [pltpu.VMEM(a.shape, a.dtype) for a in operands[:-1]]
    return pl.pallas_call(
        kernel,
        out_shape=pltpu.VMEM((members, cells), F32),
        in_specs=[hbm] * 7,
        out_specs=vmem,
        scratch_shapes=staged + [
            pltpu.SMEM(loc_level.shape, I32),
            dma((8,)),
            pltpu.VMEM((CAP, 128), F32),
            pltpu.VMEM((CAP, 128), F32),
            pltpu.VMEM((CAP * members, 128), F32),
            pltpu.VMEM((NBATCH, gauges, 128), I32),
            pltpu.VMEM((NBATCH, gauges, 128), I32),
            pltpu.VMEM((NBATCH, 4, 128), F32),
            pltpu.VMEM((NBATCH, NZ, 4, 128), F32),
            pltpu.VMEM((NBATCH, NXC, NZ, 4, 128), F32),
            pltpu.VMEM((NBATCH, NCORE, total, gauges // NCORE), F32),
            pltpu.VMEM((total, cells // NY), F32),
            pltpu.VMEM((total, cells // NY), F32),
            pltpu.VMEM((total, total), F32),
            dma((NBATCH, 7)), dma((NBATCH, 7)), dma((NBATCH, 7)), dma((NBATCH, 7)),
            dma((NBATCH, 7)), dma((NBATCH, 7)), dma((7,)), dma((7,)), dma((7,)), dma((7,)),
            dma((NBATCH, 8)), dma((NBATCH, 8)),
        ],
        compiler_params=pltpu.CompilerParams(
            collective_id=0, has_side_effects=True, vmem_limit_bytes=60 * 2**20
        ),
    )(*operands)


def solution(mesh):
    placed = (P("grp", "cells"), P(), P(), P(), P(), P(), P(None, "cells"))
    return jax.shard_map(
        local, mesh=mesh, in_specs=placed, out_specs=P("grp", "cells"), check_vma=False
    )
```

```python
import functools

import jax
import jax.numpy as jnp
from jax import lax
from jax.experimental import pallas as pl
from jax.experimental.pallas import tpu as pltpu
from jax.sharding import PartitionSpec as P

MESH = pl.DeviceIdType.MESH
F32, BF16, I32 = jnp.float32, jnp.bfloat16, jnp.int32
NBATCH = 2
NSIT = 12
CAP = 24
PIVOTS = 4
NX, NZ, NCORE = 4, 8, 2
NY = 8
NXC = NX * NCORE
FAR_FIRST = (4, 3, 5, 2, 6, 1, 7)
NEAR = (6, 5, 4, 3, 2, 1, 0)


def split2(x):
    hi = x.astype(BF16)
    lo = (x - hi.astype(F32)).astype(BF16)
    return hi, lo


def split3(x):
    hi = x.astype(BF16)
    rest = x - hi.astype(F32)
    mid = rest.astype(BF16)
    lo = (rest - mid.astype(F32)).astype(BF16)
    return hi, mid, lo


def nn(a, b):
    return lax.dot_general(a, b, (((1,), (0,)), ((), ())), preferred_element_type=F32)


def nt(a, b):
    return lax.dot_general(a, b, (((1,), (1,)), ((), ())), preferred_element_type=F32)


def iota(shape, dim):
    return lax.broadcasted_iota(I32, shape, dim)


def wide(a, x):
    ah, al = split2(a)
    xh, xl = split2(x)
    left = jnp.concatenate([ah, al], axis=1)
    return nn(left, jnp.concatenate([xh, xh], axis=0)) + nn(ah, xl)


def ranks(o_row):
    count = o_row.shape[1]
    o_col = jnp.transpose(jnp.broadcast_to(o_row, (128, count)))
    tiles = []
    for t in range(count // 128):
        same = o_col == o_row[:, t * 128 : (t + 1) * 128]
        earlier = iota((count, 128), 0) > iota((count, 128), 1) + t * 128
        tiles.append(jnp.where(same & earlier, 1.0, 0.0).astype(BF16))
    equal = jnp.concatenate(tiles, axis=1)
    rank_col = nn(equal, jnp.ones((count, 128), BF16))
    rank_row = nt(jnp.ones((8, count), BF16), equal)[0:1]
    return o_col, rank_col, rank_row


def places(o_col, rank_col):
    o = o_col.astype(I32)
    r = rank_col.astype(I32)
    tile = ((o >> 4) * NCORE + (o & 1)) * NZ + ((o >> 1) & (NZ - 1))
    return (r >> 3) * (NXC * NZ) + tile, r & 7


def compact(grid3, row, group, members):
    count = row.shape[0]
    lanes = iota((count, 128), 1)
    onehot = jnp.concatenate(
        [
            jnp.where(row == lanes + t * 128, 1.0, 0.0).astype(BF16)
            for t in range(pl.cdiv(grid3.shape[0], 128))
        ],
        axis=1,
    )[:, : grid3.shape[0]]
    picked = nn(onehot, grid3)
    keep = (lanes >> 4) == group
    kept = jnp.concatenate(
        [jnp.where(keep, picked[:, t * 128 : (t + 1) * 128], 0.0).astype(BF16) for t in range(3)],
        axis=1,
    )
    fold = jnp.where((iota((members, 384), 1) & 15) == iota((members, 384), 0), 1.0, 0.0)
    return nt(fold.astype(BF16), kept)


def gauge_taper(levels, o_row, b_row):
    count = o_row.shape[1]
    i = iota((NXC * NZ, count), 0)
    xc, z = i >> 3, i & (NZ - 1)
    owner = ((xc >> 1) * NZ + z) * NCORE + (xc & 1)
    onehot = jnp.where(owner == o_row, 1.0, 0.0).astype(BF16)
    by_block = nn(jnp.transpose(levels).astype(BF16), onehot)
    hit = iota(by_block.shape, 0) == b_row
    return jnp.sum(jnp.where(hit, by_block, 0.0), axis=0, keepdims=True)


def innovations(prior, value, error):
    members = prior.shape[0]
    ymean = jnp.sum(prior, axis=0, keepdims=True) / members
    smat = (prior - ymean) * (1.0 / (error * jnp.sqrt(jnp.float32(members - 1))))
    dvec = (value - ymean) / error
    sh, sl = split2(smat)
    both = jnp.concatenate([sh, sl], axis=0)
    top = nt(sh, both)
    low = nt(sl, both)
    gram = top[:, :members] + (top[:, members:] + low[:, :members]) + low[:, members:]
    bvec = jnp.sum(smat * dvec, axis=1, keepdims=True)
    return gram, bvec


def stacked(x):
    hi, lo = split2(x)
    row = jnp.concatenate([hi, lo], axis=1)
    return jnp.concatenate([row, row], axis=0)


def halves(x):
    return jnp.concatenate(split2(x), axis=1)


def joined(x):
    n = x.shape[1] // 2
    return x[:, :n] + x[:, n:]


def newton(eye, y, z):
    wy, wz = stacked(y), stacked(z)
    q = 1.5 * eye - 0.5 * joined(nn(halves(z), wy))
    hq = halves(q)
    return joined(nn(hq, wy)), joined(nn(hq, wz))


def sweep(m_ref, j):
    n = m_ref.shape[0]
    span = range(PIVOTS)
    lane = iota((1, n), 1)
    m = m_ref[...]
    rows = [m_ref[pl.ds(j + i, 1), :] for i in span]
    at = [lane == j + i for i in span]
    e = [[None] * PIVOTS for _ in span]
    for i in span:
        for k in range(i, PIVOTS):
            e[i][k] = e[k][i] = jnp.sum(jnp.where(at[k], rows[i], 0.0), axis=1, keepdims=True)
    cols = [jnp.sum(jnp.where(at[k], m, 0.0), axis=1, keepdims=True) for k in span]
    for q in span:
        inv = 1.0 / e[q][q]
        scaled = [e[q][k] * inv for k in span]
        new = [[None] * PIVOTS for _ in span]
        for i in span:
            for k in range(i, PIVOTS):
                if i == q and k == q:
                    v = -inv
                elif i == q or k == q:
                    v = scaled[k if i == q else i]
                else:
                    v = e[i][k] - e[i][q] * scaled[k]
                new[i][k] = new[k][i] = v
        e = new
    u = []
    for i in span:
        acc = -e[i][0] * rows[0]
        for k in range(1, PIVOTS):
            acc = acc - e[i][k] * rows[k]
        for k in span:
            acc = jnp.where(at[k], e[i][k], acc)
        u.append(acc)
    pivot = functools.reduce(jnp.logical_or, at)
    new = jnp.where(pivot, 0.0, m)
    for i in span:
        new = new - cols[i] * u[i]
    m_ref[...] = new
    for i in span:
        m_ref[pl.ds(j + i, 1), :] = u[i]


def transform(m_ref, amat, eye, stops):
    scal = jnp.sum(jnp.sum(amat * eye, axis=1, keepdims=True), axis=0, keepdims=True)
    m_ref[...] = amat
    steps = amat.shape[0] // PIVOTS
    most = NSIT - 2

    def three(i, carry):
        for k in range(3):
            sweep(m_ref, (i * 3 + k) * PIVOTS)
        return newton(eye, *carry)

    def one(i, carry):
        sweep(m_ref, (steps - NSIT + i) * PIVOTS)
        return newton(eye, *carry)

    carry, done = (amat / scal, eye), 0
    for stop, act in stops:
        carry = lax.fori_loop(done, stop, three, carry)
        act()
        done = stop
    carry = lax.fori_loop(done, most, three, carry)
    _, z = lax.fori_loop(most, NSIT, one, carry)
    return z * lax.rsqrt(scal)


def apply_mix(mixer, x, taper):
    anomaly = x - jnp.sum(x, axis=0, keepdims=True) / x.shape[0]
    return x + taper * wide(mixer, anomaly)


def kernel(
    ens_hbm, own_hbm, blk_hbm, gw_hbm, val_hbm, err_hbm, lvl_hbm, out_ref,
    ens_ref, own_ref, blk_ref, gw_ref, val_ref, err_ref, lvl_ref, cps,
    w_ref, b_ref, y_ref, row_ref, group_ref, tile_ref, line_ref, grid_ref, prior_ref, full_ref,
    mix_ref, taper_ref, m_ref, s1s, s1r, s2s, s2r, s3s, s3r, s4s, s4r, s6s, s6r,
):
    members = ens_ref.shape[0]
    gauges = blk_ref.shape[1]
    half = gauges // NCORE
    cell = lax.axis_index("cells")
    my = lax.axis_index("grp")
    core = cell % NCORE
    mz = (cell // NCORE) % NZ
    mx = cell // (NCORE * NZ)
    mxc = mx * NCORE + core

    def z_peer(d):
        return ((mx * NZ + (mz + d) % NZ) * NCORE + core, my)

    def xc_peer(d):
        xc = (mxc + d) % NXC
        return (((xc // NCORE) * NZ + mz) * NCORE + xc % NCORE, my)

    def y_peer(d):
        return (cell, (my + d) % NY)

    twin = (cell + 1 - 2 * core, my)

    barrier = pltpu.get_barrier_semaphore()
    for d in FAR_FIRST:
        for peer in (z_peer(d), xc_peer(d), y_peer(d)):
            pl.semaphore_signal(barrier, inc=1, device_id=peer, device_id_type=MESH)

    pairs = [
        (own_hbm, own_ref), (blk_hbm, blk_ref), (gw_hbm.at[0], gw_ref.at[0]), (ens_hbm, ens_ref),
        (lvl_hbm, lvl_ref), (gw_hbm.at[1], gw_ref.at[1]), (val_hbm, val_ref), (err_hbm, err_ref),
        (ens_hbm, full_ref.at[pl.ds(pl.multiple_of(my * members, members), members)]),
    ]
    staged = [pltpu.make_async_copy(a, b, cps.at[i]) for i, (a, b) in enumerate(pairs)]
    for c in staged:
        c.start()
    nblk = ens_ref.shape[1] // 128

    def readings(b):
        slot = iota((CAP, gauges), 0)
        o_row = own_ref[b]
        o_col, rank_col, rank_row = ranks(o_row.astype(F32))
        row_ref[b], group_ref[b] = places(o_col, rank_col)
        mine = (o_row == cell) & (rank_row.astype(I32) == slot)
        pick = jnp.where(mine, 1.0, 0.0).astype(BF16)
        g0, g1, g2 = split3(gw_ref[b])
        w_ref[...] = nn(pick, g0) + nn(pick, g1) + nn(pick, g2)
        blocks = jnp.broadcast_to(blk_ref[b : b + 1, :], (128, gauges)).astype(F32).astype(BF16)
        b_ref[...] = nt(pick, blocks)
        if b == 0:
            staged[3].wait()

        def reading(s, carry):
            want = b_ref[pl.ds(s, 1), :]
            got = jnp.zeros((members, 128), F32)
            for k in range(nblk):
                got = jnp.where(want == k, ens_ref[:, k * 128 : (k + 1) * 128], got)
            at = pl.ds(pl.multiple_of(s * members, members), members)
            y_ref[at, :] = got * w_ref[pl.ds(s, 1), :]
            return carry

        lax.fori_loop(0, CAP, reading, 0, unroll=4)
        y3 = jnp.concatenate(split3(y_ref[...]), axis=1)
        flat = nt(jnp.ones((8, y3.shape[1]), BF16), y3)[:4]
        sub = iota((4, 128), 0)
        lane = iota((4, 128), 1)
        tile = jnp.zeros((4, 128), F32)
        for r in range(3):
            tile = jnp.where(sub == r, flat[:, r * 128 : (r + 1) * 128], tile)
        if b == 1:
            for k in range(nblk):
                level = lvl_ref[0, k].astype(F32) * 0.25
                tile = jnp.where((sub == 3) & (lane == k), level, tile)
        tile_ref[b] = tile

    for c in staged[:3]:
        c.wait()
    readings(0)
    for c in staged[4:]:
        c.wait()

    pl.semaphore_wait(barrier, 21)

    def remote(src, dst, send, recv, peer):
        return pltpu.make_async_remote_copy(
            src_ref=src, dst_ref=dst, send_sem=send, recv_sem=recv,
            device_id=peer, device_id_type=MESH,
        )

    chunk = ens_ref.shape[1] // 2

    def rows(y):
        return pl.ds(pl.multiple_of(y * members, members), members)

    def ring(way, step, part):
        block = rows((my + (step - 1) * (NY - way)) % NY)
        half_block = pl.ds((part if way == 1 else 1 - part) * chunk, chunk)
        at = (0 if way == 1 else 1, step - 1, part)
        here = full_ref.at[block, half_block]
        return remote(here, here, s4s.at[at], s4r.at[at], (cell, (my + way) % NY))

    hops = {
        (step, part): [ring(way, step, part) for way in (1, NY - 1)]
        for step in range(1, NY // 2 + 1)
        for part in range(1 if step == NY // 2 else 2)
    }

    def arrive(step, part):
        for c in hops[step, part]:
            c.wait_recv()

    def forward(step, part):
        arrive(step - 1, part)
        for c in hops[step, part]:
            c.start()

    c1 = [
        [
            remote(
                tile_ref.at[b], line_ref.at[b, mz], s1s.at[b, d - 1], s1r.at[b, d - 1], z_peer(d)
            )
            for d in FAR_FIRST
        ]
        for b in range(NBATCH)
    ]
    for c in c1[0] + hops[1, 0]:
        c.start()
    readings(1)
    for c in c1[1] + hops[1, 1]:
        c.start()
    for b in range(NBATCH):
        line_ref[b, mz] = tile_ref[b]
    c2 = [
        [
            remote(
                line_ref.at[b], grid_ref.at[b, mxc], s2s.at[b, d - 1], s2r.at[b, d - 1], xc_peer(d)
            )
            for d in FAR_FIRST
        ]
        for b in range(NBATCH)
    ]
    c3 = [
        [
            remote(
                prior_ref.at[b, core, rows(my)], prior_ref.at[b, core, rows(my)],
                s3s.at[b, d - 1], s3r.at[b, d - 1], y_peer(d),
            )
            for d in FAR_FIRST
        ]
        for b in range(NBATCH)
    ]
    c6 = [
        [
            remote(
                prior_ref.at[b, core, rows((my + NY - d) % NY)],
                prior_ref.at[b, core, rows((my + NY - d) % NY)],
                s6s.at[b, d], s6r.at[b, d], twin,
            )
            for d in (0,) + FAR_FIRST
        ]
        for b in range(NBATCH)
    ]

    def packed(b):
        parts = [grid_ref[b, :, :, r, :].reshape(NXC * NZ, 128) for r in range(3)]
        grid3 = jnp.concatenate(split3(jnp.concatenate(parts, axis=0)), axis=1)
        mine = pl.ds(pl.multiple_of(core * half, half), half)
        prior_ref[b, core, rows(my), :] = compact(
            grid3, row_ref[b, mine, :], group_ref[b, mine, :], members
        )

    def onward(b, ranks):
        for k in ranks:
            c3[b][k].wait_recv()
            c6[b][k + 1].start()

    for b in range(NBATCH):
        for c in c1[b]:
            c.wait_recv()
        for c in c2[b]:
            c.start()
        grid_ref[b, mxc] = line_ref[b]
    forward(2, 0)
    for c in c2[0]:
        c.wait_recv()
    packed(0)
    for c in c3[0] + c6[0][:1]:
        c.start()
    for c in c2[1]:
        c.wait_recv()
    packed(1)
    levels = grid_ref[1, :, :, 3, :].reshape(NXC * NZ, 128)
    taper_g = gauge_taper(levels, own_ref[1], blk_ref[1:2, :])
    for b in range(NBATCH):
        for k in range(nblk):
            level = lvl_ref[b, k].astype(F32) * 0.25
            taper_ref[b : b + 1, k * 128 : (k + 1) * 128] = jnp.full((1, 128), level, F32)
    onward(0, NEAR[:4])
    forward(2, 1)
    onward(0, NEAR[4:])
    for c in c3[1] + c6[1][:1]:
        c.start()
    for c in c6[0]:
        c.wait_recv()

    def at_1_2():
        forward(3, 0)

    def at_1_7():
        forward(3, 1)

    def at_1_9():
        onward(1, NEAR)

    def at_2_2():
        forward(4, 0)

    stops = [[(2, at_1_2), (7, at_1_7), (9, at_1_9)], [(2, at_2_2)]]

    def prior_of(b):
        return jnp.concatenate([prior_ref[b, h] for h in range(NCORE)], axis=1)

    total = members * NY
    eye = jnp.where(iota((total, total), 0) == iota((total, total), 1), 1.0, 0.0)
    scale = 1.0 / jnp.sqrt(jnp.float32(total - 1))
    prior = prior_of(0)
    for b in range(NBATCH):
        gram, bvec = innovations(prior, val_ref[b : b + 1, :], err_ref[b : b + 1, :])
        amat = eye + gram
        dmat = transform(m_ref, amat, eye, stops[b]) - eye
        w_row = -jnp.sum(m_ref[...] * bvec, axis=0, keepdims=True)
        mixer = dmat + w_row * scale
        mix_ref[b] = mixer
        if b == 0:
            for c in c6[1]:
                c.wait_recv()
            centred = mixer - jnp.sum(mixer, axis=0, keepdims=True) / total
            prior = apply_mix(mixer, prior_of(1), taper_g)
    own = [mix_ref[b, rows(my), :] for b in range(NBATCH)]
    stack = jnp.concatenate(own + [wide(own[1], centred)], axis=0)
    hi, lo = split2(stack)
    left = jnp.concatenate([hi, lo], axis=1)
    for step, part in hops:
        if (step + 1, part) not in hops:
            arrive(step, part)
    width = 512
    for i in range(ens_ref.shape[1] // width):
        at = slice(i * width, (i + 1) * width)
        x = full_ref[:, at]
        xh, xl = split2(x - jnp.sum(x, axis=0, keepdims=True) / total)
        both = nn(left, jnp.concatenate([xh, xh], axis=0)) + nn(hi, xl)
        t0, t1 = taper_ref[0:1, at], taper_ref[1:2, at]
        first, second, third = (both[k * members : (k + 1) * members] for k in range(3))
        out_ref[:, at] = ens_ref[:, at] + t0 * first + t1 * (second + t0 * third)
    sent = [c for group in hops.values() for c in group]
    for c in c1[0] + c1[1] + c2[0] + c2[1] + c3[0] + c3[1] + c6[0] + c6[1] + sent:
        c.wait_send()


def local(ensemble, gauge_owner, gauge_block, gauge_weight, gauge_value, gauge_error, loc_level):
    members, cells = ensemble.shape
    gauges = gauge_block.shape[1]
    vmem = pl.BlockSpec(memory_space=pltpu.VMEM)
    hbm = pl.BlockSpec(memory_space=pltpu.HBM)
    dma = pltpu.SemaphoreType.DMA
    total = members * NY
    operands = (
        ensemble, jnp.swapaxes(gauge_owner, 1, 2), gauge_block, gauge_weight, gauge_value,
        gauge_error, loc_level,
    )
    staged = [pltpu.VMEM(a.shape, a.dtype) for a in operands[:-1]]
    return pl.pallas_call(
        kernel,
        out_shape=pltpu.VMEM((members, cells), F32),
        in_specs=[hbm] * 7,
        out_specs=vmem,
        scratch_shapes=staged + [
            pltpu.SMEM(loc_level.shape, I32),
            dma((9,)),
            pltpu.VMEM((CAP, 128), F32),
            pltpu.VMEM((CAP, 128), F32),
            pltpu.VMEM((CAP * members, 128), F32),
            pltpu.VMEM((NBATCH, gauges, 128), I32),
            pltpu.VMEM((NBATCH, gauges, 128), I32),
            pltpu.VMEM((NBATCH, 4, 128), F32),
            pltpu.VMEM((NBATCH, NZ, 4, 128), F32),
            pltpu.VMEM((NBATCH, NXC, NZ, 4, 128), F32),
            pltpu.VMEM((NBATCH, NCORE, total, gauges // NCORE), F32),
            pltpu.VMEM((total, cells), F32),
            pltpu.VMEM((NBATCH, total, total), F32),
            pltpu.VMEM((NBATCH, cells), F32),
            pltpu.VMEM((total, total), F32),
            dma((NBATCH, 7)), dma((NBATCH, 7)), dma((NBATCH, 7)), dma((NBATCH, 7)),
            dma((NBATCH, 7)), dma((NBATCH, 7)), dma((2, 4, 2)), dma((2, 4, 2)),
            dma((NBATCH, 8)), dma((NBATCH, 8)),
        ],
        compiler_params=pltpu.CompilerParams(
            collective_id=0, has_side_effects=True, vmem_limit_bytes=60 * 2**20
        ),
    )(*operands)


def solution(mesh):
    placed = (P("grp", "cells"), P(), P(), P(), P(), P(), P(None, "cells"))
    return jax.shard_map(
        local, mesh=mesh, in_specs=placed, out_specs=P("grp", "cells"), check_vma=False
    )
```

```python
import functools

import jax
import jax.numpy as jnp
from jax import lax
from jax.experimental import pallas as pl
from jax.experimental.pallas import tpu as pltpu
from jax.sharding import PartitionSpec as P

MESH = pl.DeviceIdType.MESH
F32, BF16, I32 = jnp.float32, jnp.bfloat16, jnp.int32
NBATCH = 2
NSIT = 12
CAP = 24
PIVOTS = 4
NX, NZ, NCORE = 4, 8, 2
NY = 8
NXC = NX * NCORE
FAR_FIRST = (4, 3, 5, 2, 6, 1, 7)
NEAR = (6, 5, 4, 3, 2, 1, 0)


def split2(x):
    hi = x.astype(BF16)
    lo = (x - hi.astype(F32)).astype(BF16)
    return hi, lo


def split3(x):
    hi = x.astype(BF16)
    rest = x - hi.astype(F32)
    mid = rest.astype(BF16)
    lo = (rest - mid.astype(F32)).astype(BF16)
    return hi, mid, lo


def nn(a, b):
    return lax.dot_general(a, b, (((1,), (0,)), ((), ())), preferred_element_type=F32)


def nt(a, b):
    return lax.dot_general(a, b, (((1,), (1,)), ((), ())), preferred_element_type=F32)


def iota(shape, dim):
    return lax.broadcasted_iota(I32, shape, dim)


def wide(a, x):
    ah, al = split2(a)
    xh, xl = split2(x)
    left = jnp.concatenate([ah, al], axis=1)
    return nn(left, jnp.concatenate([xh, xh], axis=0)) + nn(ah, xl)


def ranks(o_row):
    count = o_row.shape[1]
    o_col = jnp.transpose(jnp.broadcast_to(o_row, (128, count)))
    tiles = []
    for t in range(count // 128):
        same = o_col == o_row[:, t * 128 : (t + 1) * 128]
        earlier = iota((count, 128), 0) > iota((count, 128), 1) + t * 128
        tiles.append(jnp.where(same & earlier, 1.0, 0.0).astype(BF16))
    equal = jnp.concatenate(tiles, axis=1)
    rank_col = nn(equal, jnp.ones((count, 128), BF16))
    rank_row = nt(jnp.ones((8, count), BF16), equal)[0:1]
    return o_col, rank_col, rank_row


def places(o_col, rank_col):
    o = o_col.astype(I32)
    r = rank_col.astype(I32)
    tile = ((o >> 4) * NCORE + (o & 1)) * NZ + ((o >> 1) & (NZ - 1))
    return (r >> 3) * (NXC * NZ) + tile, r & 7


def compact(grid3, row, group, members):
    count = row.shape[0]
    lanes = iota((count, 128), 1)
    onehot = jnp.concatenate(
        [
            jnp.where(row == lanes + t * 128, 1.0, 0.0).astype(BF16)
            for t in range(pl.cdiv(grid3.shape[0], 128))
        ],
        axis=1,
    )[:, : grid3.shape[0]]
    picked = nn(onehot, grid3)
    keep = (lanes >> 4) == group
    kept = jnp.concatenate(
        [jnp.where(keep, picked[:, t * 128 : (t + 1) * 128], 0.0).astype(BF16) for t in range(3)],
        axis=1,
    )
    fold = jnp.where((iota((members, 384), 1) & 15) == iota((members, 384), 0), 1.0, 0.0)
    return nt(fold.astype(BF16), kept)


def gauge_taper(levels, o_row, b_row):
    count = o_row.shape[1]
    i = iota((NXC * NZ, count), 0)
    xc, z = i >> 3, i & (NZ - 1)
    owner = ((xc >> 1) * NZ + z) * NCORE + (xc & 1)
    onehot = jnp.where(owner == o_row, 1.0, 0.0).astype(BF16)
    by_block = nn(jnp.transpose(levels).astype(BF16), onehot)
    hit = iota(by_block.shape, 0) == b_row
    return jnp.sum(jnp.where(hit, by_block, 0.0), axis=0, keepdims=True)


def innovations(prior, value, error):
    members = prior.shape[0]
    ymean = jnp.sum(prior, axis=0, keepdims=True) / members
    smat = (prior - ymean) * (1.0 / (error * jnp.sqrt(jnp.float32(members - 1))))
    dvec = (value - ymean) / error
    sh, sl = split2(smat)
    both = jnp.concatenate([sh, sl], axis=0)
    top = nt(sh, both)
    low = nt(sl, both)
    gram = top[:, :members] + (top[:, members:] + low[:, :members]) + low[:, members:]
    bvec = jnp.sum(smat * dvec, axis=1, keepdims=True)
    return gram, bvec


def stacked(x):
    hi, lo = split2(x)
    row = jnp.concatenate([hi, lo], axis=1)
    return jnp.concatenate([row, row], axis=0)


def halves(x):
    return jnp.concatenate(split2(x), axis=1)


def joined(x):
    n = x.shape[1] // 2
    return x[:, :n] + x[:, n:]


def newton(eye, y, z):
    wy, wz = stacked(y), stacked(z)
    q = 1.5 * eye - 0.5 * joined(nn(halves(z), wy))
    hq = halves(q)
    return joined(nn(hq, wy)), joined(nn(hq, wz))


def sweep(m_ref, j):
    n = m_ref.shape[0]
    span = range(PIVOTS)
    lane = iota((1, n), 1)
    m = m_ref[...]
    rows = [m_ref[pl.ds(j + i, 1), :] for i in span]
    at = [lane == j + i for i in span]
    e = [[None] * PIVOTS for _ in span]
    for i in span:
        for k in range(i, PIVOTS):
            e[i][k] = e[k][i] = jnp.sum(jnp.where(at[k], rows[i], 0.0), axis=1, keepdims=True)
    cols = [jnp.sum(jnp.where(at[k], m, 0.0), axis=1, keepdims=True) for k in span]
    for q in span:
        inv = 1.0 / e[q][q]
        scaled = [e[q][k] * inv for k in span]
        new = [[None] * PIVOTS for _ in span]
        for i in span:
            for k in range(i, PIVOTS):
                if i == q and k == q:
                    v = -inv
                elif i == q or k == q:
                    v = scaled[k if i == q else i]
                else:
                    v = e[i][k] - e[i][q] * scaled[k]
                new[i][k] = new[k][i] = v
        e = new
    u = []
    for i in span:
        acc = -e[i][0] * rows[0]
        for k in range(1, PIVOTS):
            acc = acc - e[i][k] * rows[k]
        for k in span:
            acc = jnp.where(at[k], e[i][k], acc)
        u.append(acc)
    pivot = functools.reduce(jnp.logical_or, at)
    new = jnp.where(pivot, 0.0, m)
    for i in span:
        new = new - cols[i] * u[i]
    m_ref[...] = new
    for i in span:
        m_ref[pl.ds(j + i, 1), :] = u[i]


def transform(m_ref, amat, eye, stops):
    scal = jnp.sum(jnp.sum(amat * eye, axis=1, keepdims=True), axis=0, keepdims=True)
    m_ref[...] = amat
    most = amat.shape[0] // PIVOTS - 2 * NSIT

    def several(count, offset):
        def step(i, carry):
            for k in range(count):
                sweep(m_ref, (i * count + k + offset) * PIVOTS)
            return newton(eye, *carry)

        return step

    carry, done = (amat / scal, eye), 0
    for stop, act in stops + [(NSIT, lambda: None)]:
        if done < most:
            carry = lax.fori_loop(done, min(stop, most), several(3, 0), carry)
        if stop > most:
            carry = lax.fori_loop(max(done, most), stop, several(2, most), carry)
        act()
        done = stop
    _, z = carry
    return z * lax.rsqrt(scal)


def apply_mix(mixer, x, taper):
    anomaly = x - jnp.sum(x, axis=0, keepdims=True) / x.shape[0]
    return x + taper * wide(mixer, anomaly)


def kernel(
    ens_hbm, own_hbm, blk_hbm, gw_hbm, val_hbm, err_hbm, lvl_hbm, out_ref,
    ens_ref, own_ref, blk_ref, gw_ref, val_ref, err_ref, lvl_ref, cps,
    w_ref, b_ref, y_ref, row_ref, group_ref, tile_ref, line_ref, grid_ref, prior_ref, full_ref,
    mix_ref, taper_ref, m_ref, s1s, s1r, s2s, s2r, s3s, s3r, s4s, s4r, s6s, s6r,
):
    members = ens_ref.shape[0]
    gauges = blk_ref.shape[1]
    half = gauges // NCORE
    cell = lax.axis_index("cells")
    my = lax.axis_index("grp")
    core = cell % NCORE
    mz = (cell // NCORE) % NZ
    mx = cell // (NCORE * NZ)
    mxc = mx * NCORE + core

    def z_peer(d):
        return ((mx * NZ + (mz + d) % NZ) * NCORE + core, my)

    def xc_peer(d):
        xc = (mxc + d) % NXC
        return (((xc // NCORE) * NZ + mz) * NCORE + xc % NCORE, my)

    def y_peer(d):
        return (cell, (my + d) % NY)

    twin = (cell + 1 - 2 * core, my)

    barrier = pltpu.get_barrier_semaphore()
    for peer_of in (z_peer, y_peer, xc_peer):
        for d in FAR_FIRST:
            pl.semaphore_signal(barrier, inc=1, device_id=peer_of(d), device_id_type=MESH)

    pairs = [
        (own_hbm, own_ref), (blk_hbm, blk_ref), (gw_hbm.at[0], gw_ref.at[0]), (ens_hbm, ens_ref),
        (lvl_hbm, lvl_ref), (gw_hbm.at[1], gw_ref.at[1]), (val_hbm, val_ref), (err_hbm, err_ref),
        (ens_hbm, full_ref.at[pl.ds(pl.multiple_of(my * members, members), members)]),
    ]
    staged = [pltpu.make_async_copy(a, b, cps.at[i]) for i, (a, b) in enumerate(pairs)]
    for c in staged:
        c.start()
    nblk = ens_ref.shape[1] // 128

    def readings(b):
        slot = iota((CAP, gauges), 0)
        o_row = own_ref[b]
        o_col, rank_col, rank_row = ranks(o_row.astype(F32))
        row_ref[b], group_ref[b] = places(o_col, rank_col)
        mine = (o_row == cell) & (rank_row.astype(I32) == slot)
        pick = jnp.where(mine, 1.0, 0.0).astype(BF16)
        g0, g1, g2 = split3(gw_ref[b])
        w_ref[...] = nn(pick, g0) + nn(pick, g1) + nn(pick, g2)
        blocks = jnp.broadcast_to(blk_ref[b : b + 1, :], (128, gauges)).astype(F32).astype(BF16)
        b_ref[...] = nt(pick, blocks)
        if b == 0:
            staged[3].wait()

        def reading(s, carry):
            want = b_ref[pl.ds(s, 1), :]
            got = jnp.zeros((members, 128), F32)
            for k in range(nblk):
                got = jnp.where(want == k, ens_ref[:, k * 128 : (k + 1) * 128], got)
            at = pl.ds(pl.multiple_of(s * members, members), members)
            y_ref[at, :] = got * w_ref[pl.ds(s, 1), :]
            return carry

        lax.fori_loop(0, CAP, reading, 0, unroll=4)
        y3 = jnp.concatenate(split3(y_ref[...]), axis=1)
        flat = nt(jnp.ones((8, y3.shape[1]), BF16), y3)[:4]
        sub = iota((4, 128), 0)
        lane = iota((4, 128), 1)
        tile = jnp.zeros((4, 128), F32)
        for r in range(3):
            tile = jnp.where(sub == r, flat[:, r * 128 : (r + 1) * 128], tile)
        if b == 1:
            for k in range(nblk):
                level = lvl_ref[0, k].astype(F32) * 0.25
                tile = jnp.where((sub == 3) & (lane == k), level, tile)
        tile_ref[b] = tile

    for c in staged[:3]:
        c.wait()
    readings(0)
    for c in staged[4:]:
        c.wait()

    pl.semaphore_wait(barrier, 21)

    def remote(src, dst, send, recv, peer):
        return pltpu.make_async_remote_copy(
            src_ref=src, dst_ref=dst, send_sem=send, recv_sem=recv,
            device_id=peer, device_id_type=MESH,
        )

    chunk = ens_ref.shape[1] // 2

    def rows(y):
        return pl.ds(pl.multiple_of(y * members, members), members)

    def ring(way, step, part):
        block = rows((my + (step - 1) * (NY - way)) % NY)
        half_block = pl.ds((part if way == 1 else 1 - part) * chunk, chunk)
        at = (0 if way == 1 else 1, step - 1, part)
        here = full_ref.at[block, half_block]
        return remote(here, here, s4s.at[at], s4r.at[at], (cell, (my + way) % NY))

    hops = {
        (step, part): [ring(way, step, part) for way in (1, NY - 1)]
        for step in range(1, NY // 2 + 1)
        for part in range(1 if step == NY // 2 else 2)
    }

    def arrive(step, part):
        for c in hops[step, part]:
            c.wait_recv()

    def forward(step, part):
        arrive(step - 1, part)
        for c in hops[step, part]:
            c.start()

    c1 = [
        [
            remote(
                tile_ref.at[b], line_ref.at[b, mz], s1s.at[b, d - 1], s1r.at[b, d - 1], z_peer(d)
            )
            for d in FAR_FIRST
        ]
        for b in range(NBATCH)
    ]
    for c in c1[0] + hops[1, 0]:
        c.start()
    readings(1)
    for c in c1[1] + hops[1, 1]:
        c.start()
    for b in range(NBATCH):
        line_ref[b, mz] = tile_ref[b]
    c2 = [
        [
            remote(
                line_ref.at[b], grid_ref.at[b, mxc], s2s.at[b, d - 1], s2r.at[b, d - 1], xc_peer(d)
            )
            for d in FAR_FIRST
        ]
        for b in range(NBATCH)
    ]
    c3 = [
        [
            remote(
                prior_ref.at[b, core, rows(my)], prior_ref.at[b, core, rows(my)],
                s3s.at[b, d - 1], s3r.at[b, d - 1], y_peer(d),
            )
            for d in FAR_FIRST
        ]
        for b in range(NBATCH)
    ]
    c6 = [
        [
            remote(
                prior_ref.at[b, core, rows((my + NY - d) % NY)],
                prior_ref.at[b, core, rows((my + NY - d) % NY)],
                s6s.at[b, d], s6r.at[b, d], twin,
            )
            for d in (0,) + FAR_FIRST
        ]
        for b in range(NBATCH)
    ]

    def packed(b):
        parts = [grid_ref[b, :, :, r, :].reshape(NXC * NZ, 128) for r in range(3)]
        grid3 = jnp.concatenate(split3(jnp.concatenate(parts, axis=0)), axis=1)
        mine = pl.ds(pl.multiple_of(core * half, half), half)
        prior_ref[b, core, rows(my), :] = compact(
            grid3, row_ref[b, mine, :], group_ref[b, mine, :], members
        )

    def onward(b, ranks):
        for k in ranks:
            c3[b][k].wait_recv()
            c6[b][k + 1].start()

    for b in range(NBATCH):
        for c in c1[b]:
            c.wait_recv()
        for c in c2[b]:
            c.start()
        grid_ref[b, mxc] = line_ref[b]
    forward(2, 0)
    forward(2, 1)
    for c in c2[0]:
        c.wait_recv()
    packed(0)
    for c in c3[0] + c6[0][:1]:
        c.start()
    for c in c2[1]:
        c.wait_recv()
    packed(1)
    levels = grid_ref[1, :, :, 3, :].reshape(NXC * NZ, 128)
    taper_g = gauge_taper(levels, own_ref[1], blk_ref[1:2, :])
    for b in range(NBATCH):
        for k in range(nblk):
            level = lvl_ref[b, k].astype(F32) * 0.25
            taper_ref[b : b + 1, k * 128 : (k + 1) * 128] = jnp.full((1, 128), level, F32)
    onward(0, NEAR[:4])
    onward(0, NEAR[4:])
    for c in c3[1] + c6[1][:1]:
        c.start()
    for c in c6[0]:
        c.wait_recv()

    def at_1_1():
        forward(3, 0)

    def at_1_5():
        forward(3, 1)

    def at_1_9():
        onward(1, NEAR)

    def at_1_10():
        forward(4, 0)

    stops = [[(1, at_1_1), (5, at_1_5), (9, at_1_9), (10, at_1_10)], []]

    def prior_of(b):
        return jnp.concatenate([prior_ref[b, h] for h in range(NCORE)], axis=1)

    total = members * NY
    eye = jnp.where(iota((total, total), 0) == iota((total, total), 1), 1.0, 0.0)
    scale = 1.0 / jnp.sqrt(jnp.float32(total - 1))
    prior = prior_of(0)
    for b in range(NBATCH):
        gram, bvec = innovations(prior, val_ref[b : b + 1, :], err_ref[b : b + 1, :])
        amat = eye + gram
        dmat = transform(m_ref, amat, eye, stops[b]) - eye
        w_row = -jnp.sum(m_ref[...] * bvec, axis=0, keepdims=True)
        mixer = dmat + w_row * scale
        mix_ref[b] = mixer
        if b == 0:
            for c in c6[1]:
                c.wait_recv()
            centred = mixer - jnp.sum(mixer, axis=0, keepdims=True) / total
            prior = apply_mix(mixer, prior_of(1), taper_g)
    own = [mix_ref[b, rows(my), :] for b in range(NBATCH)]
    stack = jnp.concatenate(own + [wide(own[1], centred)], axis=0)
    hi, lo = split2(stack)
    left = jnp.concatenate([hi, lo], axis=1)
    for step, part in hops:
        if (step + 1, part) not in hops:
            arrive(step, part)
    width = 512
    for i in range(ens_ref.shape[1] // width):
        at = slice(i * width, (i + 1) * width)
        x = full_ref[:, at]
        xh, xl = split2(x - jnp.sum(x, axis=0, keepdims=True) / total)
        both = nn(left, jnp.concatenate([xh, xh], axis=0)) + nn(hi, xl)
        t0, t1 = taper_ref[0:1, at], taper_ref[1:2, at]
        first, second, third = (both[k * members : (k + 1) * members] for k in range(3))
        out_ref[:, at] = ens_ref[:, at] + t0 * first + t1 * (second + t0 * third)
    sent = [c for group in hops.values() for c in group]
    for c in c1[0] + c1[1] + c2[0] + c2[1] + c3[0] + c3[1] + c6[0] + c6[1] + sent:
        c.wait_send()


def local(ensemble, gauge_owner, gauge_block, gauge_weight, gauge_value, gauge_error, loc_level):
    members, cells = ensemble.shape
    gauges = gauge_block.shape[1]
    vmem = pl.BlockSpec(memory_space=pltpu.VMEM)
    hbm = pl.BlockSpec(memory_space=pltpu.HBM)
    dma = pltpu.SemaphoreType.DMA
    total = members * NY
    operands = (
        ensemble, jnp.swapaxes(gauge_owner, 1, 2), gauge_block, gauge_weight, gauge_value,
        gauge_error, loc_level,
    )
    staged = [pltpu.VMEM(a.shape, a.dtype) for a in operands[:-1]]
    return pl.pallas_call(
        kernel,
        out_shape=pltpu.VMEM((members, cells), F32),
        in_specs=[hbm] * 7,
        out_specs=vmem,
        scratch_shapes=staged + [
            pltpu.SMEM(loc_level.shape, I32),
            dma((9,)),
            pltpu.VMEM((CAP, 128), F32),
            pltpu.VMEM((CAP, 128), F32),
            pltpu.VMEM((CAP * members, 128), F32),
            pltpu.VMEM((NBATCH, gauges, 128), I32),
            pltpu.VMEM((NBATCH, gauges, 128), I32),
            pltpu.VMEM((NBATCH, 4, 128), F32),
            pltpu.VMEM((NBATCH, NZ, 4, 128), F32),
            pltpu.VMEM((NBATCH, NXC, NZ, 4, 128), F32),
            pltpu.VMEM((NBATCH, NCORE, total, gauges // NCORE), F32),
            pltpu.VMEM((total, cells), F32),
            pltpu.VMEM((NBATCH, total, total), F32),
            pltpu.VMEM((NBATCH, cells), F32),
            pltpu.VMEM((total, total), F32),
            dma((NBATCH, 7)), dma((NBATCH, 7)), dma((NBATCH, 7)), dma((NBATCH, 7)),
            dma((NBATCH, 7)), dma((NBATCH, 7)), dma((2, 4, 2)), dma((2, 4, 2)),
            dma((NBATCH, 8)), dma((NBATCH, 8)),
        ],
        compiler_params=pltpu.CompilerParams(
            collective_id=0, has_side_effects=True, vmem_limit_bytes=60 * 2**20
        ),
    )(*operands)


def solution(mesh):
    placed = (P("grp", "cells"), P(), P(), P(), P(), P(), P(None, "cells"))
    return jax.shard_map(
        local, mesh=mesh, in_specs=placed, out_specs=P("grp", "cells"), check_vma=False
    )
```

```python
import functools

import jax
import jax.numpy as jnp
from jax import lax
from jax.experimental import pallas as pl
from jax.experimental.pallas import tpu as pltpu
from jax.sharding import PartitionSpec as P

MESH = pl.DeviceIdType.MESH
F32, BF16, I32 = jnp.float32, jnp.bfloat16, jnp.int32
NBATCH = 2
NSIT = 12
CAP = 24
PIVOTS = 4
NX, NZ, NCORE = 4, 8, 2
NY = 8
NXC = NX * NCORE
FAR_FIRST = (4, 3, 5, 2, 6, 1, 7)
NEAR = (6, 5, 4, 3, 2, 1, 0)


def split2(x):
    hi = x.astype(BF16)
    lo = (x - hi.astype(F32)).astype(BF16)
    return hi, lo


def split3(x):
    hi = x.astype(BF16)
    rest = x - hi.astype(F32)
    mid = rest.astype(BF16)
    lo = (rest - mid.astype(F32)).astype(BF16)
    return hi, mid, lo


def nn(a, b):
    return lax.dot_general(a, b, (((1,), (0,)), ((), ())), preferred_element_type=F32)


def nt(a, b):
    return lax.dot_general(a, b, (((1,), (1,)), ((), ())), preferred_element_type=F32)


def iota(shape, dim):
    return lax.broadcasted_iota(I32, shape, dim)


def wide(a, x):
    ah, al = split2(a)
    xh, xl = split2(x)
    left = jnp.concatenate([ah, al], axis=1)
    return nn(left, jnp.concatenate([xh, xh], axis=0)) + nn(ah, xl)


def ranks(o_row):
    count = o_row.shape[1]
    o_col = jnp.transpose(jnp.broadcast_to(o_row, (128, count)))
    tiles = []
    for t in range(count // 128):
        same = o_col == o_row[:, t * 128 : (t + 1) * 128]
        earlier = iota((count, 128), 0) > iota((count, 128), 1) + t * 128
        tiles.append(jnp.where(same & earlier, 1.0, 0.0).astype(BF16))
    equal = jnp.concatenate(tiles, axis=1)
    rank_col = nn(equal, jnp.ones((count, 128), BF16))
    rank_row = nt(jnp.ones((8, count), BF16), equal)[0:1]
    return o_col, rank_col, rank_row


def places(o_col, rank_col):
    o = o_col.astype(I32)
    r = rank_col.astype(I32)
    tile = ((o >> 4) * NCORE + (o & 1)) * NZ + ((o >> 1) & (NZ - 1))
    return (r >> 3) * (NXC * NZ) + tile, r & 7


def selectors(row, group, members):
    lanes = iota((row.shape[0], 128), 1)
    held = 3 * NXC * NZ
    onehot = jnp.concatenate(
        [jnp.where(row == lanes + t * 128, 1.0, 0.0).astype(BF16) for t in range(pl.cdiv(held, 128))],
        axis=1,
    )[:, :held]
    fold = jnp.where((iota((members, 384), 1) & 15) == iota((members, 384), 0), 1.0, 0.0)
    return onehot, jnp.where((lanes >> 4) == group, 1.0, 0.0), fold.astype(BF16)


def compact(grid3, onehot, keep, fold):
    picked = nn(onehot, grid3)
    kept = jnp.concatenate(
        [(keep * picked[:, t * 128 : (t + 1) * 128]).astype(BF16) for t in range(3)], axis=1
    )
    return nt(fold, kept)


def gauge_taper(levels, o_row, b_row):
    count = o_row.shape[1]
    i = iota((NXC * NZ, count), 0)
    xc, z = i >> 3, i & (NZ - 1)
    owner = ((xc >> 1) * NZ + z) * NCORE + (xc & 1)
    onehot = jnp.where(owner == o_row, 1.0, 0.0).astype(BF16)
    by_block = nn(jnp.transpose(levels).astype(BF16), onehot)
    hit = iota(by_block.shape, 0) == b_row
    return jnp.sum(jnp.where(hit, by_block, 0.0), axis=0, keepdims=True)


def innovations(prior, value, error):
    members = prior.shape[0]
    ymean = jnp.sum(prior, axis=0, keepdims=True) / members
    smat = (prior - ymean) * (1.0 / (error * jnp.sqrt(jnp.float32(members - 1))))
    dvec = (value - ymean) / error
    sh, sl = split2(smat)
    both = jnp.concatenate([sh, sl], axis=0)
    top = nt(sh, both)
    low = nt(sl, both)
    gram = top[:, :members] + (top[:, members:] + low[:, :members]) + low[:, members:]
    bvec = jnp.sum(smat * dvec, axis=1, keepdims=True)
    return gram, bvec


def stacked(x):
    hi, lo = split2(x)
    row = jnp.concatenate([hi, lo], axis=1)
    return jnp.concatenate([row, row], axis=0)


def halves(x):
    return jnp.concatenate(split2(x), axis=1)


def joined(x):
    n = x.shape[1] // 2
    return x[:, :n] + x[:, n:]


def newton(eye, y, z):
    wy, wz = stacked(y), stacked(z)
    q = 1.5 * eye - 0.5 * joined(nn(halves(z), wy))
    hq = halves(q)
    return joined(nn(hq, wy)), joined(nn(hq, wz))


def sweep(m_ref, j, low):
    n = m_ref.shape[0]
    span = range(PIVOTS)
    lane = iota((1, n), 1)
    m = m_ref[low:, :]
    rows = [m_ref[pl.ds(j + i, 1), :] for i in span]
    at = [lane == j + i for i in span]
    e = [[None] * PIVOTS for _ in span]
    for i in span:
        for k in range(i, PIVOTS):
            e[i][k] = e[k][i] = jnp.sum(jnp.where(at[k], rows[i], 0.0), axis=1, keepdims=True)
    cols = [jnp.sum(jnp.where(at[k], m, 0.0), axis=1, keepdims=True) for k in span]
    for q in span:
        inv = 1.0 / e[q][q]
        scaled = [e[q][k] * inv for k in span]
        new = [[None] * PIVOTS for _ in span]
        for i in span:
            for k in range(i, PIVOTS):
                if i == q and k == q:
                    v = -inv
                elif i == q or k == q:
                    v = scaled[k if i == q else i]
                else:
                    v = e[i][k] - e[i][q] * scaled[k]
                new[i][k] = new[k][i] = v
        e = new
    u = []
    for i in span:
        acc = -e[i][0] * rows[0]
        for k in range(1, PIVOTS):
            acc = acc - e[i][k] * rows[k]
        for k in span:
            acc = jnp.where(at[k], e[i][k], acc)
        u.append(acc)
    pivot = functools.reduce(jnp.logical_or, at)
    new = jnp.where(pivot, 0.0, m)
    for i in span:
        new = new - cols[i] * u[i]
    m_ref[low:, :] = new
    for i in span:
        m_ref[pl.ds(j + i, 1), :] = u[i]


def transform(m_ref, amat, eye, stops):
    scal = jnp.sum(jnp.sum(amat * eye, axis=1, keepdims=True), axis=0, keepdims=True)
    m_ref[...] = amat
    half = amat.shape[0] // 2
    most = half // (2 * PIVOTS)

    def several(count, low):
        def step(i, carry):
            for k in range(count):
                sweep(m_ref, low + ((i - (most if low else 0)) * count + k) * PIVOTS, low)
            return newton(eye, *carry)

        return step

    carry, done = (amat / scal, eye), 0
    for stop, act in stops + [(NSIT, lambda: None)]:
        if done < most:
            carry = lax.fori_loop(done, min(stop, most), several(2, 0), carry)
        if stop > most:
            carry = lax.fori_loop(max(done, most), stop, several(4, half), carry)
        act()
        done = stop
    _, z = carry
    return z * lax.rsqrt(scal)


def solved(m_ref, eye, bvec):
    half = m_ref.shape[0] // 2
    b_row = jnp.sum(eye * bvec, axis=0, keepdims=True)
    second = -jnp.sum(m_ref[half:, :] * b_row, axis=1, keepdims=True)
    second_row = jnp.sum(eye[half:] * second, axis=0, keepdims=True)
    mixed = jnp.where(iota(b_row.shape, 1) < half, b_row, second_row)
    first = -jnp.sum(m_ref[:half, :] * mixed, axis=1, keepdims=True)
    return second_row + jnp.sum(eye[:half] * first, axis=0, keepdims=True)


def apply_mix(mixer, x, taper):
    anomaly = x - jnp.sum(x, axis=0, keepdims=True) / x.shape[0]
    return x + taper * wide(mixer, anomaly)


def kernel(
    ens_hbm, own_hbm, blk_hbm, gw_hbm, val_hbm, err_hbm, lvl_hbm, out_ref,
    ens_ref, own_ref, blk_ref, gw_ref, val_ref, err_ref, lvl_ref, cps,
    w_ref, b_ref, y_ref, row_ref, group_ref, tile_ref, line_ref, grid_ref, prior_ref, full_ref,
    mix_ref, taper_ref, m_ref, s1s, s1r, s2s, s2r, s3s, s3r, s4s, s4r, s6s, s6r,
):
    members = ens_ref.shape[0]
    gauges = blk_ref.shape[1]
    half = gauges // NCORE
    cell = lax.axis_index("cells")
    my = lax.axis_index("grp")
    core = cell % NCORE
    mz = (cell // NCORE) % NZ
    mx = cell // (NCORE * NZ)
    mxc = mx * NCORE + core

    def z_peer(d):
        return ((mx * NZ + (mz + d) % NZ) * NCORE + core, my)

    def xc_peer(d):
        xc = (mxc + d) % NXC
        return (((xc // NCORE) * NZ + mz) * NCORE + xc % NCORE, my)

    def y_peer(d):
        return (cell, (my + d) % NY)

    twin = (cell + 1 - 2 * core, my)

    barrier = pltpu.get_barrier_semaphore()
    for peer_of in (z_peer, y_peer, xc_peer):
        for d in FAR_FIRST:
            pl.semaphore_signal(barrier, inc=1, device_id=peer_of(d), device_id_type=MESH)

    pairs = [
        (own_hbm, own_ref), (blk_hbm, blk_ref), (gw_hbm.at[0], gw_ref.at[0]), (ens_hbm, ens_ref),
        (lvl_hbm, lvl_ref), (gw_hbm.at[1], gw_ref.at[1]), (val_hbm, val_ref), (err_hbm, err_ref),
        (ens_hbm, full_ref.at[pl.ds(pl.multiple_of(my * members, members), members)]),
    ]
    staged = [pltpu.make_async_copy(a, b, cps.at[i]) for i, (a, b) in enumerate(pairs)]
    for c in staged:
        c.start()
    nblk = ens_ref.shape[1] // 128

    def readings(b):
        slot = iota((CAP, gauges), 0)
        o_row = own_ref[b]
        o_col, rank_col, rank_row = ranks(o_row.astype(F32))
        row_ref[b], group_ref[b] = places(o_col, rank_col)
        mine = (o_row == cell) & (rank_row.astype(I32) == slot)
        pick = jnp.where(mine, 1.0, 0.0).astype(BF16)
        if b == 0:
            staged[2].wait()
        g0, g1, g2 = split3(gw_ref[b])
        w_ref[...] = nn(pick, g0) + nn(pick, g1) + nn(pick, g2)
        blocks = jnp.broadcast_to(blk_ref[b : b + 1, :], (128, gauges)).astype(F32).astype(BF16)
        b_ref[...] = nt(pick, blocks)
        if b == 0:
            staged[3].wait()

        def reading(s, carry):
            want = b_ref[pl.ds(s, 1), :]
            got = jnp.zeros((members, 128), F32)
            for k in range(nblk):
                got = jnp.where(want == k, ens_ref[:, k * 128 : (k + 1) * 128], got)
            at = pl.ds(pl.multiple_of(s * members, members), members)
            y_ref[at, :] = got * w_ref[pl.ds(s, 1), :]
            return carry

        lax.fori_loop(0, CAP, reading, 0, unroll=4)
        y3 = jnp.concatenate(split3(y_ref[...]), axis=1)
        flat = nt(jnp.ones((8, y3.shape[1]), BF16), y3)[:4]
        sub = iota((4, 128), 0)
        lane = iota((4, 128), 1)
        tile = jnp.zeros((4, 128), F32)
        for r in range(3):
            tile = jnp.where(sub == r, flat[:, r * 128 : (r + 1) * 128], tile)
        if b == 1:
            for k in range(nblk):
                level = lvl_ref[0, k].astype(F32) * 0.25
                tile = jnp.where((sub == 3) & (lane == k), level, tile)
        tile_ref[b] = tile

    for c in staged[:2]:
        c.wait()
    readings(0)
    for c in staged[4:]:
        c.wait()

    pl.semaphore_wait(barrier, 21)

    def remote(src, dst, send, recv, peer):
        return pltpu.make_async_remote_copy(
            src_ref=src, dst_ref=dst, send_sem=send, recv_sem=recv,
            device_id=peer, device_id_type=MESH,
        )

    chunk = ens_ref.shape[1] // 2

    def rows(y):
        return pl.ds(pl.multiple_of(y * members, members), members)

    def ring(way, step, part):
        block = rows((my + (step - 1) * (NY - way)) % NY)
        half_block = pl.ds((part if way == 1 else 1 - part) * chunk, chunk)
        at = (0 if way == 1 else 1, step - 1, part)
        here = full_ref.at[block, half_block]
        return remote(here, here, s4s.at[at], s4r.at[at], (cell, (my + way) % NY))

    hops = {
        (step, part): [ring(way, step, part) for way in (1, NY - 1)]
        for step in range(1, NY // 2 + 1)
        for part in range(1 if step == NY // 2 else 2)
    }

    def arrive(step, part):
        for c in hops[step, part]:
            c.wait_recv()

    def forward(step, part):
        arrive(step - 1, part)
        for c in hops[step, part]:
            c.start()

    c1 = [
        [
            remote(
                tile_ref.at[b], line_ref.at[b, mz], s1s.at[b, d - 1], s1r.at[b, d - 1], z_peer(d)
            )
            for d in FAR_FIRST
        ]
        for b in range(NBATCH)
    ]
    for c in c1[0] + hops[1, 0]:
        c.start()
    readings(1)
    for c in c1[1] + hops[1, 1]:
        c.start()
    for b in range(NBATCH):
        line_ref[b, mz] = tile_ref[b]
    c2 = [
        [
            remote(
                line_ref.at[b], grid_ref.at[b, mxc], s2s.at[b, d - 1], s2r.at[b, d - 1], xc_peer(d)
            )
            for d in FAR_FIRST
        ]
        for b in range(NBATCH)
    ]
    c3 = [
        [
            remote(
                prior_ref.at[b, core, rows(my)], prior_ref.at[b, core, rows(my)],
                s3s.at[b, d - 1], s3r.at[b, d - 1], y_peer(d),
            )
            for d in FAR_FIRST
        ]
        for b in range(NBATCH)
    ]
    c6 = [
        [
            remote(
                prior_ref.at[b, core, rows((my + NY - d) % NY)],
                prior_ref.at[b, core, rows((my + NY - d) % NY)],
                s6s.at[b, d], s6r.at[b, d], twin,
            )
            for d in (0,) + FAR_FIRST
        ]
        for b in range(NBATCH)
    ]

    def choice(b):
        mine = pl.ds(pl.multiple_of(core * half, half), half)
        return selectors(row_ref[b, mine, :], group_ref[b, mine, :], members)

    def packed(b, chosen):
        parts = [grid_ref[b, :, :, r, :].reshape(NXC * NZ, 128) for r in range(3)]
        grid3 = jnp.concatenate(split3(jnp.concatenate(parts, axis=0)), axis=1)
        prior_ref[b, core, rows(my), :] = compact(grid3, *chosen)

    def onward(b, ranks):
        for k in ranks:
            c3[b][k].wait_recv()
            c6[b][k + 1].start()

    for b in range(NBATCH):
        for c in c1[b]:
            c.wait_recv()
        for c in c2[b]:
            c.start()
        grid_ref[b, mxc] = line_ref[b]
    chosen = choice(0)
    forward(2, 0)
    forward(2, 1)
    for c in c2[0]:
        c.wait_recv()
    packed(0, chosen)
    for c in c3[0] + c6[0][:1]:
        c.start()
    for c in c2[1]:
        c.wait_recv()
    packed(1, choice(1))
    levels = grid_ref[1, :, :, 3, :].reshape(NXC * NZ, 128)
    taper_g = gauge_taper(levels, own_ref[1], blk_ref[1:2, :])
    for b in range(NBATCH):
        for k in range(nblk):
            level = lvl_ref[b, k].astype(F32) * 0.25
            taper_ref[b : b + 1, k * 128 : (k + 1) * 128] = jnp.full((1, 128), level, F32)
    onward(0, NEAR[:4])
    onward(0, NEAR[4:])
    for c in c3[1] + c6[1][:1]:
        c.start()
    forward(3, 0)
    for c in c6[0]:
        c.wait_recv()

    def at_1_4():
        forward(3, 1)

    def at_1_9():
        onward(1, NEAR)
        forward(4, 0)

    stops = [[(4, at_1_4), (9, at_1_9)], []]

    def prior_of(b):
        return jnp.concatenate([prior_ref[b, h] for h in range(NCORE)], axis=1)

    total = members * NY
    eye = jnp.where(iota((total, total), 0) == iota((total, total), 1), 1.0, 0.0)
    scale = 1.0 / jnp.sqrt(jnp.float32(total - 1))
    prior = prior_of(0)
    for b in range(NBATCH):
        gram, bvec = innovations(prior, val_ref[b : b + 1, :], err_ref[b : b + 1, :])
        amat = eye + gram
        dmat = transform(m_ref, amat, eye, stops[b]) - eye
        w_row = solved(m_ref, eye, bvec)
        mixer = dmat + w_row * scale
        mix_ref[b] = mixer
        if b == 0:
            for c in c6[1]:
                c.wait_recv()
            centred = mixer - jnp.sum(mixer, axis=0, keepdims=True) / total
            prior = apply_mix(mixer, prior_of(1), taper_g)
    own = [mix_ref[b, rows(my), :] for b in range(NBATCH)]
    stack = jnp.concatenate(own + [wide(own[1], centred)], axis=0)
    hi, lo = split2(stack)
    left = jnp.concatenate([hi, lo], axis=1)
    for step, part in hops:
        if (step + 1, part) not in hops:
            arrive(step, part)
    width = 512
    for i in range(ens_ref.shape[1] // width):
        at = slice(i * width, (i + 1) * width)
        x = full_ref[:, at]
        xh, xl = split2(x - jnp.sum(x, axis=0, keepdims=True) / total)
        both = nn(left, jnp.concatenate([xh, xh], axis=0)) + nn(hi, xl)
        t0, t1 = taper_ref[0:1, at], taper_ref[1:2, at]
        first, second, third = (both[k * members : (k + 1) * members] for k in range(3))
        out_ref[:, at] = ens_ref[:, at] + t0 * first + t1 * (second + t0 * third)
    sent = [c for group in hops.values() for c in group]
    for c in c1[0] + c1[1] + c2[0] + c2[1] + c3[0] + c3[1] + c6[0] + c6[1] + sent:
        c.wait_send()


def local(ensemble, gauge_owner, gauge_block, gauge_weight, gauge_value, gauge_error, loc_level):
    members, cells = ensemble.shape
    gauges = gauge_block.shape[1]
    vmem = pl.BlockSpec(memory_space=pltpu.VMEM)
    hbm = pl.BlockSpec(memory_space=pltpu.HBM)
    dma = pltpu.SemaphoreType.DMA
    total = members * NY
    operands = (
        ensemble, jnp.swapaxes(gauge_owner, 1, 2), gauge_block, gauge_weight, gauge_value,
        gauge_error, loc_level,
    )
    staged = [pltpu.VMEM(a.shape, a.dtype) for a in operands[:-1]]
    return pl.pallas_call(
        kernel,
        out_shape=pltpu.VMEM((members, cells), F32),
        in_specs=[hbm] * 7,
        out_specs=vmem,
        scratch_shapes=staged + [
            pltpu.SMEM(loc_level.shape, I32),
            dma((9,)),
            pltpu.VMEM((CAP, 128), F32),
            pltpu.VMEM((CAP, 128), F32),
            pltpu.VMEM((CAP * members, 128), F32),
            pltpu.VMEM((NBATCH, gauges, 128), I32),
            pltpu.VMEM((NBATCH, gauges, 128), I32),
            pltpu.VMEM((NBATCH, 4, 128), F32),
            pltpu.VMEM((NBATCH, NZ, 4, 128), F32),
            pltpu.VMEM((NBATCH, NXC, NZ, 4, 128), F32),
            pltpu.VMEM((NBATCH, NCORE, total, gauges // NCORE), F32),
            pltpu.VMEM((total, cells), F32),
            pltpu.VMEM((NBATCH, total, total), F32),
            pltpu.VMEM((NBATCH, cells), F32),
            pltpu.VMEM((total, total), F32),
            dma((NBATCH, 7)), dma((NBATCH, 7)), dma((NBATCH, 7)), dma((NBATCH, 7)),
            dma((NBATCH, 7)), dma((NBATCH, 7)), dma((2, 4, 2)), dma((2, 4, 2)),
            dma((NBATCH, 8)), dma((NBATCH, 8)),
        ],
        compiler_params=pltpu.CompilerParams(
            collective_id=0, has_side_effects=True, vmem_limit_bytes=60 * 2**20
        ),
    )(*operands)


def solution(mesh):
    placed = (P("grp", "cells"), P(), P(), P(), P(), P(), P(None, "cells"))
    return jax.shard_map(
        local, mesh=mesh, in_specs=placed, out_specs=P("grp", "cells"), check_vma=False
    )
```

```python
import functools

import jax
import jax.numpy as jnp
from jax import lax
from jax.experimental import pallas as pl
from jax.experimental.pallas import tpu as pltpu
from jax.sharding import PartitionSpec as P

MESH = pl.DeviceIdType.MESH
F32, BF16, I32 = jnp.float32, jnp.bfloat16, jnp.int32
NBATCH = 2
NSIT = 12
CAP = 24
PIVOTS = 4
NX, NZ, NCORE = 4, 8, 2
NY = 8
NXC = NX * NCORE
FAR_FIRST = (4, 3, 5, 2, 6, 1, 7)
NEAR = (6, 5, 4, 3, 2, 1, 0)


def split2(x):
    hi = x.astype(BF16)
    lo = (x - hi.astype(F32)).astype(BF16)
    return hi, lo


def split3(x):
    hi = x.astype(BF16)
    rest = x - hi.astype(F32)
    mid = rest.astype(BF16)
    lo = (rest - mid.astype(F32)).astype(BF16)
    return hi, mid, lo


def nn(a, b):
    return lax.dot_general(a, b, (((1,), (0,)), ((), ())), preferred_element_type=F32)


def nt(a, b):
    return lax.dot_general(a, b, (((1,), (1,)), ((), ())), preferred_element_type=F32)


def iota(shape, dim):
    return lax.broadcasted_iota(I32, shape, dim)


def wide(a, x):
    ah, al = split2(a)
    xh, xl = split2(x)
    left = jnp.concatenate([ah, al], axis=1)
    return nn(left, jnp.concatenate([xh, xh], axis=0)) + nn(ah, xl)


def ranks(o_row):
    count = o_row.shape[1]
    o_col = jnp.transpose(jnp.broadcast_to(o_row, (128, count)))
    tiles = []
    for t in range(count // 128):
        same = o_col == o_row[:, t * 128 : (t + 1) * 128]
        earlier = iota((count, 128), 0) > iota((count, 128), 1) + t * 128
        tiles.append(jnp.where(same & earlier, 1.0, 0.0).astype(BF16))
    equal = jnp.concatenate(tiles, axis=1)
    rank_col = nn(equal, jnp.ones((count, 128), BF16))
    rank_row = nt(jnp.ones((8, count), BF16), equal)[0:1]
    return o_col, rank_col, rank_row


def places(o_col, rank_col):
    o = o_col.astype(I32)
    r = rank_col.astype(I32)
    tile = ((o >> 4) * NCORE + (o & 1)) * NZ + ((o >> 1) & (NZ - 1))
    return (r >> 3) * (NXC * NZ) + tile, r & 7


def selectors(row, group, members):
    lanes = iota((row.shape[0], 128), 1)
    held = 3 * NXC * NZ
    onehot = jnp.concatenate(
        [jnp.where(row == lanes + t * 128, 1.0, 0.0).astype(BF16) for t in range(pl.cdiv(held, 128))],
        axis=1,
    )[:, :held]
    fold = jnp.where((iota((members, 384), 1) & 15) == iota((members, 384), 0), 1.0, 0.0)
    return onehot, jnp.where((lanes >> 4) == group, 1.0, 0.0), fold.astype(BF16)


def compact(grid3, onehot, keep, fold):
    picked = nn(onehot, grid3)
    kept = jnp.concatenate(
        [(keep * picked[:, t * 128 : (t + 1) * 128]).astype(BF16) for t in range(3)], axis=1
    )
    return nt(fold, kept)


def gauge_taper(levels, o_row, b_row):
    count = o_row.shape[1]
    i = iota((NXC * NZ, count), 0)
    xc, z = i >> 3, i & (NZ - 1)
    owner = ((xc >> 1) * NZ + z) * NCORE + (xc & 1)
    onehot = jnp.where(owner == o_row, 1.0, 0.0).astype(BF16)
    by_block = nn(jnp.transpose(levels).astype(BF16), onehot)
    hit = iota(by_block.shape, 0) == b_row
    return jnp.sum(jnp.where(hit, by_block, 0.0), axis=0, keepdims=True)


def innovations(prior, shift, value, error):
    members = prior.shape[0]
    ymean = jnp.sum(prior, axis=0, keepdims=True) / members
    smat = (prior - ymean) * (1.0 / (error * jnp.sqrt(jnp.float32(members - 1))))
    dvec = (value - (ymean + shift)) / error
    sh, sl = split2(smat)
    both = jnp.concatenate([sh, sl], axis=0)
    top = nt(sh, both)
    low = nt(sl, both)
    gram = top[:, :members] + (top[:, members:] + low[:, :members]) + low[:, members:]
    bvec = jnp.sum(smat * dvec, axis=1, keepdims=True)
    return gram, bvec


def stacked(x):
    hi, lo = split2(x)
    row = jnp.concatenate([hi, lo], axis=1)
    return jnp.concatenate([row, row], axis=0)


def halves(x):
    return jnp.concatenate(split2(x), axis=1)


def joined(x):
    n = x.shape[1] // 2
    return x[:, :n] + x[:, n:]


def newton(eye, y, z):
    wy, wz = stacked(y), stacked(z)
    q = 1.5 * eye - 0.5 * joined(nn(halves(z), wy))
    hq = halves(q)
    return joined(nn(hq, wy)), joined(nn(hq, wz))


def sweep(m_ref, j, low):
    n = m_ref.shape[0]
    span = range(PIVOTS)
    lane = iota((1, n), 1)
    m = m_ref[low:, :]
    rows = [m_ref[pl.ds(j + i, 1), :] for i in span]
    at = [lane == j + i for i in span]
    e = [[None] * PIVOTS for _ in span]
    for i in span:
        for k in range(i, PIVOTS):
            e[i][k] = e[k][i] = jnp.sum(jnp.where(at[k], rows[i], 0.0), axis=1, keepdims=True)
    cols = [jnp.sum(jnp.where(at[k], m, 0.0), axis=1, keepdims=True) for k in span]
    for q in span:
        inv = 1.0 / e[q][q]
        scaled = [e[q][k] * inv for k in span]
        new = [[None] * PIVOTS for _ in span]
        for i in span:
            for k in range(i, PIVOTS):
                if i == q and k == q:
                    v = -inv
                elif i == q or k == q:
                    v = scaled[k if i == q else i]
                else:
                    v = e[i][k] - e[i][q] * scaled[k]
                new[i][k] = new[k][i] = v
        e = new
    u = []
    for i in span:
        acc = -e[i][0] * rows[0]
        for k in range(1, PIVOTS):
            acc = acc - e[i][k] * rows[k]
        for k in span:
            acc = jnp.where(at[k], e[i][k], acc)
        u.append(acc)
    pivot = functools.reduce(jnp.logical_or, at)
    new = jnp.where(pivot, 0.0, m)
    for i in span:
        new = new - cols[i] * u[i]
    m_ref[low:, :] = new
    for i in span:
        m_ref[pl.ds(j + i, 1), :] = u[i]


def transform(m_ref, amat, eye, stops):
    scal = jnp.sum(jnp.sum(amat * eye, axis=1, keepdims=True), axis=0, keepdims=True)
    m_ref[...] = amat
    half = amat.shape[0] // 2
    most = half // (2 * PIVOTS)

    def several(count, low):
        def step(i, carry):
            for k in range(count):
                sweep(m_ref, low + ((i - (most if low else 0)) * count + k) * PIVOTS, low)
            return newton(eye, *carry)

        return step

    carry, done = (amat / scal, eye), 0
    for stop, act in stops + [(NSIT, lambda: None)]:
        if done < most:
            carry = lax.fori_loop(done, min(stop, most), several(2, 0), carry)
        if stop > most:
            carry = lax.fori_loop(max(done, most), stop, several(4, half), carry)
        act()
        done = stop
    _, z = carry
    return z * lax.rsqrt(scal)


def solved(m_ref, eye, bvec):
    half = m_ref.shape[0] // 2
    b_row = jnp.sum(eye * bvec, axis=0, keepdims=True)
    second = -jnp.sum(m_ref[half:, :] * b_row, axis=1, keepdims=True)
    second_row = jnp.sum(eye[half:] * second, axis=0, keepdims=True)
    mixed = jnp.where(iota(b_row.shape, 1) < half, b_row, second_row)
    first = -jnp.sum(m_ref[:half, :] * mixed, axis=1, keepdims=True)
    row = second_row + jnp.sum(eye[:half] * first, axis=0, keepdims=True)
    return row, jnp.concatenate([first, second], axis=0)


def apply_mix(mixer, x, taper):
    anomaly = x - jnp.sum(x, axis=0, keepdims=True) / x.shape[0]
    return x + taper * wide(mixer, anomaly)


def kernel(
    ens_hbm, own_hbm, blk_hbm, gw_hbm, val_hbm, err_hbm, lvl_hbm, out_ref,
    ens_ref, own_ref, blk_ref, gw_ref, val_ref, err_ref, lvl_ref, cps,
    w_ref, b_ref, y_ref, row_ref, group_ref, tile_ref, line_ref, grid_ref, prior_ref, full_ref,
    mix_ref, taper_ref, m_ref, s1s, s1r, s2s, s2r, s3s, s3r, s4s, s4r, s6s, s6r,
):
    members = ens_ref.shape[0]
    gauges = blk_ref.shape[1]
    half = gauges // NCORE
    cell = lax.axis_index("cells")
    my = lax.axis_index("grp")
    core = cell % NCORE
    mz = (cell // NCORE) % NZ
    mx = cell // (NCORE * NZ)
    mxc = mx * NCORE + core

    def z_peer(d):
        return ((mx * NZ + (mz + d) % NZ) * NCORE + core, my)

    def xc_peer(d):
        xc = (mxc + d) % NXC
        return (((xc // NCORE) * NZ + mz) * NCORE + xc % NCORE, my)

    def y_peer(d):
        return (cell, (my + d) % NY)

    twin = (cell + 1 - 2 * core, my)

    barrier = pltpu.get_barrier_semaphore()
    for peer_of in (z_peer, y_peer, xc_peer):
        for d in FAR_FIRST:
            pl.semaphore_signal(barrier, inc=1, device_id=peer_of(d), device_id_type=MESH)

    pairs = [
        (own_hbm, own_ref), (blk_hbm, blk_ref), (gw_hbm.at[0], gw_ref.at[0]), (ens_hbm, ens_ref),
        (lvl_hbm, lvl_ref), (gw_hbm.at[1], gw_ref.at[1]), (val_hbm, val_ref), (err_hbm, err_ref),
        (ens_hbm, full_ref.at[pl.ds(pl.multiple_of(my * members, members), members)]),
    ]
    staged = [pltpu.make_async_copy(a, b, cps.at[i]) for i, (a, b) in enumerate(pairs)]
    for c in staged:
        c.start()
    nblk = ens_ref.shape[1] // 128

    def readings(b):
        slot = iota((CAP, gauges), 0)
        o_row = own_ref[b]
        o_col, rank_col, rank_row = ranks(o_row.astype(F32))
        row_ref[b], group_ref[b] = places(o_col, rank_col)
        mine = (o_row == cell) & (rank_row.astype(I32) == slot)
        pick = jnp.where(mine, 1.0, 0.0).astype(BF16)
        if b == 0:
            staged[2].wait()
        g0, g1, g2 = split3(gw_ref[b])
        w_ref[...] = nn(pick, g0) + nn(pick, g1) + nn(pick, g2)
        blocks = jnp.broadcast_to(blk_ref[b : b + 1, :], (128, gauges)).astype(F32).astype(BF16)
        b_ref[...] = nt(pick, blocks)
        if b == 0:
            staged[3].wait()

        def reading(s, carry):
            want = b_ref[pl.ds(s, 1), :]
            got = jnp.zeros((members, 128), F32)
            for k in range(nblk):
                got = jnp.where(want == k, ens_ref[:, k * 128 : (k + 1) * 128], got)
            at = pl.ds(pl.multiple_of(s * members, members), members)
            y_ref[at, :] = got * w_ref[pl.ds(s, 1), :]
            return carry

        lax.fori_loop(0, CAP, reading, 0, unroll=4)
        y3 = jnp.concatenate(split3(y_ref[...]), axis=1)
        flat = nt(jnp.ones((8, y3.shape[1]), BF16), y3)[:4]
        sub = iota((4, 128), 0)
        lane = iota((4, 128), 1)
        tile = jnp.zeros((4, 128), F32)
        for r in range(3):
            tile = jnp.where(sub == r, flat[:, r * 128 : (r + 1) * 128], tile)
        if b == 1:
            for k in range(nblk):
                level = lvl_ref[0, k].astype(F32) * 0.25
                tile = jnp.where((sub == 3) & (lane == k), level, tile)
        tile_ref[b] = tile

    for c in staged[:2]:
        c.wait()
    readings(0)
    for c in staged[4:]:
        c.wait()

    pl.semaphore_wait(barrier, 21)

    def remote(src, dst, send, recv, peer):
        return pltpu.make_async_remote_copy(
            src_ref=src, dst_ref=dst, send_sem=send, recv_sem=recv,
            device_id=peer, device_id_type=MESH,
        )

    chunk = ens_ref.shape[1] // 2

    def rows(y):
        return pl.ds(pl.multiple_of(y * members, members), members)

    def ring(way, step, part):
        block = rows((my + (step - 1) * (NY - way)) % NY)
        half_block = pl.ds((part if way == 1 else 1 - part) * chunk, chunk)
        at = (0 if way == 1 else 1, step - 1, part)
        here = full_ref.at[block, half_block]
        return remote(here, here, s4s.at[at], s4r.at[at], (cell, (my + way) % NY))

    hops = {
        (step, part): [ring(way, step, part) for way in (1, NY - 1)]
        for step in range(1, NY // 2 + 1)
        for part in range(1 if step == NY // 2 else 2)
    }

    def arrive(step, part):
        for c in hops[step, part]:
            c.wait_recv()

    def forward(step, part):
        arrive(step - 1, part)
        for c in hops[step, part]:
            c.start()

    c1 = [
        [
            remote(
                tile_ref.at[b], line_ref.at[b, mz], s1s.at[b, d - 1], s1r.at[b, d - 1], z_peer(d)
            )
            for d in FAR_FIRST
        ]
        for b in range(NBATCH)
    ]
    for c in c1[0] + hops[1, 0]:
        c.start()
    readings(1)
    for c in c1[1] + hops[1, 1]:
        c.start()
    for b in range(NBATCH):
        line_ref[b, mz] = tile_ref[b]
    c2 = [
        [
            remote(
                line_ref.at[b], grid_ref.at[b, mxc], s2s.at[b, d - 1], s2r.at[b, d - 1], xc_peer(d)
            )
            for d in FAR_FIRST
        ]
        for b in range(NBATCH)
    ]
    c3 = [
        [
            remote(
                prior_ref.at[b, core, rows(my)], prior_ref.at[b, core, rows(my)],
                s3s.at[b, d - 1], s3r.at[b, d - 1], y_peer(d),
            )
            for d in FAR_FIRST
        ]
        for b in range(NBATCH)
    ]
    c6 = [
        [
            remote(
                prior_ref.at[b, core, rows((my + NY - d) % NY)],
                prior_ref.at[b, core, rows((my + NY - d) % NY)],
                s6s.at[b, d], s6r.at[b, d], twin,
            )
            for d in (0,) + FAR_FIRST
        ]
        for b in range(NBATCH)
    ]

    def choice(b):
        mine = pl.ds(pl.multiple_of(core * half, half), half)
        return selectors(row_ref[b, mine, :], group_ref[b, mine, :], members)

    def packed(b, chosen):
        parts = [grid_ref[b, :, :, r, :].reshape(NXC * NZ, 128) for r in range(3)]
        grid3 = jnp.concatenate(split3(jnp.concatenate(parts, axis=0)), axis=1)
        prior_ref[b, core, rows(my), :] = compact(grid3, *chosen)

    def onward(b, ranks):
        for k in ranks:
            c3[b][k].wait_recv()
            c6[b][k + 1].start()

    for b in range(NBATCH):
        for c in c1[b]:
            c.wait_recv()
        for c in c2[b]:
            c.start()
        grid_ref[b, mxc] = line_ref[b]
    chosen = choice(0)
    forward(2, 0)
    forward(2, 1)
    for c in c2[0]:
        c.wait_recv()
    packed(0, chosen)
    for c in c3[0] + c6[0][:1]:
        c.start()
    for c in c2[1]:
        c.wait_recv()
    packed(1, choice(1))
    levels = grid_ref[1, :, :, 3, :].reshape(NXC * NZ, 128)
    taper_g = gauge_taper(levels, own_ref[1], blk_ref[1:2, :])
    for b in range(NBATCH):
        for k in range(nblk):
            level = lvl_ref[b, k].astype(F32) * 0.25
            taper_ref[b : b + 1, k * 128 : (k + 1) * 128] = jnp.full((1, 128), level, F32)
    onward(0, NEAR[:4])
    onward(0, NEAR[4:])
    for c in c3[1] + c6[1][:1]:
        c.start()
    forward(3, 0)
    for c in c6[0]:
        c.wait_recv()

    def at_1_4():
        forward(3, 1)

    def at_1_9():
        onward(1, NEAR)
        forward(4, 0)

    stops = [[(4, at_1_4), (9, at_1_9)], []]

    def prior_of(b):
        return jnp.concatenate([prior_ref[b, h] for h in range(NCORE)], axis=1)

    total = members * NY
    eye = jnp.where(iota((total, total), 0) == iota((total, total), 1), 1.0, 0.0)
    scale = 1.0 / jnp.sqrt(jnp.float32(total - 1))
    prior, shift = prior_of(0), 0.0
    for b in range(NBATCH):
        gram, bvec = innovations(prior, shift, val_ref[b : b + 1, :], err_ref[b : b + 1, :])
        amat = eye + gram
        dmat = transform(m_ref, amat, eye, stops[b]) - eye
        w_row, w_col = solved(m_ref, eye, bvec)
        mixer = dmat + w_row * scale
        mix_ref[b] = mixer
        if b == 0:
            for c in c6[1]:
                c.wait_recv()
            centred = mixer - jnp.sum(mixer, axis=0, keepdims=True) / total
            before = prior_of(1)
            prior = apply_mix(dmat, before, taper_g)
            apart = before - jnp.sum(before, axis=0, keepdims=True) / total
            shift = taper_g * (scale * jnp.sum(w_col * apart, axis=0, keepdims=True))
    own = [mix_ref[b, rows(my), :] for b in range(NBATCH)]
    stack = jnp.concatenate(own + [wide(own[1], centred)], axis=0)
    hi, lo = split2(stack)
    left = jnp.concatenate([hi, lo], axis=1)
    for step, part in hops:
        if (step + 1, part) not in hops:
            arrive(step, part)
    width = 512
    for i in range(ens_ref.shape[1] // width):
        at = slice(i * width, (i + 1) * width)
        x = full_ref[:, at]
        xh, xl = split2(x - jnp.sum(x, axis=0, keepdims=True) / total)
        both = nn(left, jnp.concatenate([xh, xh], axis=0)) + nn(hi, xl)
        t0, t1 = taper_ref[0:1, at], taper_ref[1:2, at]
        first, second, third = (both[k * members : (k + 1) * members] for k in range(3))
        out_ref[:, at] = ens_ref[:, at] + t0 * first + t1 * (second + t0 * third)
    sent = [c for group in hops.values() for c in group]
    for c in c1[0] + c1[1] + c2[0] + c2[1] + c3[0] + c3[1] + c6[0] + c6[1] + sent:
        c.wait_send()


def local(ensemble, gauge_owner, gauge_block, gauge_weight, gauge_value, gauge_error, loc_level):
    members, cells = ensemble.shape
    gauges = gauge_block.shape[1]
    vmem = pl.BlockSpec(memory_space=pltpu.VMEM)
    hbm = pl.BlockSpec(memory_space=pltpu.HBM)
    dma = pltpu.SemaphoreType.DMA
    total = members * NY
    operands = (
        ensemble, jnp.swapaxes(gauge_owner, 1, 2), gauge_block, gauge_weight, gauge_value,
        gauge_error, loc_level,
    )
    staged = [pltpu.VMEM(a.shape, a.dtype) for a in operands[:-1]]
    return pl.pallas_call(
        kernel,
        out_shape=pltpu.VMEM((members, cells), F32),
        in_specs=[hbm] * 7,
        out_specs=vmem,
        scratch_shapes=staged + [
            pltpu.SMEM(loc_level.shape, I32),
            dma((9,)),
            pltpu.VMEM((CAP, 128), F32),
            pltpu.VMEM((CAP, 128), F32),
            pltpu.VMEM((CAP * members, 128), F32),
            pltpu.VMEM((NBATCH, gauges, 128), I32),
            pltpu.VMEM((NBATCH, gauges, 128), I32),
            pltpu.VMEM((NBATCH, 4, 128), F32),
            pltpu.VMEM((NBATCH, NZ, 4, 128), F32),
            pltpu.VMEM((NBATCH, NXC, NZ, 4, 128), F32),
            pltpu.VMEM((NBATCH, NCORE, total, gauges // NCORE), F32),
            pltpu.VMEM((total, cells), F32),
            pltpu.VMEM((NBATCH, total, total), F32),
            pltpu.VMEM((NBATCH, cells), F32),
            pltpu.VMEM((total, total), F32),
            dma((NBATCH, 7)), dma((NBATCH, 7)), dma((NBATCH, 7)), dma((NBATCH, 7)),
            dma((NBATCH, 7)), dma((NBATCH, 7)), dma((2, 4, 2)), dma((2, 4, 2)),
            dma((NBATCH, 8)), dma((NBATCH, 8)),
        ],
        compiler_params=pltpu.CompilerParams(
            collective_id=0, has_side_effects=True, vmem_limit_bytes=60 * 2**20
        ),
    )(*operands)


def solution(mesh):
    placed = (P("grp", "cells"), P(), P(), P(), P(), P(), P(None, "cells"))
    return jax.shard_map(
        local, mesh=mesh, in_specs=placed, out_specs=P("grp", "cells"), check_vma=False
    )
```
